512 devices in a mesh: gx: 128 (over x, z, y_lo), gy: 4 (over y_hi, core).
Axes of the slice: x: 4, y: 8 (y_hi: 2, y_lo: 4; y = y_hi * 4 + y_lo), z: 8, core: 2. Of those that a mesh axis runs over, the one named last changes fastest.
Arguments:
- tangent: float32 [8, 5, 512, 16, 128], P(None, None, 'gx', 'gy'), may hold values from -6 to 6
- base_state: float32 [5, 512, 16, 128], P(None, 'gx', 'gy'), may hold values from -0.5 to 4, as said below
- shock_flags: int32 [128, 4, 32], P('gx', 'gy'), may hold values from 0 to 1, as said below
Outputs:
- tangent_out: float32 [8, 5, 512, 16, 128], P(None, None, 'gx', 'gy')
The draws below stay inside these ranges and needn't reach their ends.
Inputs may be any that keep to these rules, and one draw needn't show every extreme that they name: `base_state`: every node holds a state with density from 0.6 to 1.4 and pressure above 0.5. `shock_flags`: every block of 1 x 1 x 32 elements of one device holds at least one and at most 16 flagged elements; some block holds exactly 16.
All inputs are finite; a program needn't handle non-finite values.
Results may differ from the reference program's by a relative error of at most 0.0001.
Values sent between devices are 32-bit elements; how exact they have to be, the bound alone decides.
No kernel may reach another device: no remote copies, remote signals or barrier semaphores. Data moves between devices by JAX's collectives and lax.ppermute only.
A program may use at most 64 MiB of HBM per device.

```python
import math
import jax
import jax.numpy as jnp
import numpy as np
from jax import lax

EX = 1
EY = 1
EZ = 32
COLS = 8
NXE = 128
NYE = 4
NXN = 512
NYN = 16
NZN = 128
FMOST = 16


def draw_base_state(key, part):
    key = jax.random.fold_in(key, 11)
    keys = jax.random.split(key, 6)
    amp_lo, amp_hi, speed_lo, speed_hi = (0.08, 0.3, 0.2, 0.8)
    amplitude = jnp.exp(jax.random.uniform(keys[0], (NXE, NYE, EZ), jnp.float32, jnp.log(amp_lo), jnp.log(amp_hi)))
    amplitude = jnp.repeat(jnp.repeat(jnp.repeat(amplitude, 4, axis=0), 4, axis=1), 4, axis=2)
    shape_nodes = (NXN, NYN, NZN)
    density = 1.0 + amplitude * jax.random.uniform(keys[1], shape_nodes, jnp.float32, -1.0, 1.0)
    stream = jax.random.uniform(keys[2], shape_nodes, jnp.float32, speed_lo, speed_hi)
    radial = jax.random.uniform(keys[3], shape_nodes, jnp.float32, -0.2, 0.2)
    spanwise = jax.random.uniform(keys[4], shape_nodes, jnp.float32, -0.2, 0.2)
    pressure = 1.0 / 1.4 * (1.0 + jax.random.uniform(keys[5], shape_nodes, jnp.float32, -0.2, 0.2))
    energy = pressure / 0.4 + 0.5 * density * (stream * stream + radial * radial + spanwise * spanwise)
    return jnp.stack([density, density * stream, density * radial, density * spanwise, energy]).astype(jnp.float32)


def draw_shock_flags(key, part):
    key = jax.random.fold_in(key, 23)
    keys = jax.random.split(key, 4)
    blocks_x = NXE // EX
    blocks_y = NYE // EY
    devices = blocks_x * blocks_y
    block_size = EX * EY * EZ
    drawn_count = jax.random.randint(keys[0], (devices,), 1, FMOST + 1)
    chosen = jax.random.randint(keys[2], (), 0, devices)
    counts = jnp.where(jnp.arange(devices) == chosen, FMOST, drawn_count)
    scores = jax.random.randint(keys[3], (devices, block_size), 0, 4096) * block_size + jnp.arange(block_size)[None, :]
    ordering = jnp.argsort(scores, axis=1)
    rank_of = jnp.argsort(ordering, axis=1)
    flagged = (rank_of < counts[:, None]).astype(jnp.int32)
    flagged = flagged.reshape(blocks_x, blocks_y, EX, EY, EZ).transpose(0, 2, 1, 3, 4)
    return flagged.reshape(NXE, NYE, EZ)


def block_levels(rng, extent, shards, smallest, high):
    def one(axis_at, blocks):
        draws = jax.random.uniform(jax.random.fold_in(jax.random.fold_in(rng, 6), axis_at), (blocks,), jnp.float32, smallest / len(shards), high / len(shards))
        return jnp.repeat(jnp.exp(draws), extent[axis_at] // blocks).reshape((-1,) + (1,) * (len(extent) - axis_at - 1))

    level = one(*shards[0])
    for cut in shards[1:]:
        level = level * one(*cut)
    return level


def centred(own_key, extent, deviation, limit, cuts=(), dtype=jnp.bfloat16):
    array = jax.random.normal(own_key, extent, jnp.float32) * deviation
    if len(cuts) > 0:
        array = block_levels(own_key, extent, cuts, -0.22, 0.18) * array
    return jnp.clip(array, min=-limit, max=limit).astype(dtype)


def setup_inputs(seed: int = 0) -> dict:
    key_list = jax.random.split(jax.random.key(seed), 4)
    return {
        "tangent": centred(key_list[0], (COLS, 5, NXN, NYN, NZN), 1.0, 6.0, ((2, 128), (3, 4)), jnp.float32),
        "base_state": draw_base_state(jax.random.fold_in(key_list[3], 71), 0),
        "shock_flags": draw_shock_flags(jax.random.fold_in(key_list[3], 71), 0),
    }


GAMMA_MINUS = 0.4
STEP = 0.1
EPS_TOP = 0.1
SENSOR_MID = -2.3
SENSOR_WIDTH = 0.5
END_PENALTY = 6.0

def legendre_values(x):
    return [1.0, x, 0.5 * (3.0 * x * x - 1.0), 0.5 * (5.0 * x * x * x - 3.0 * x)]

def node_tables():
    inner_point = math.sqrt(0.2)
    points = [-1.0, -inner_point, inner_point, 1.0]
    weights = [1.0 / 6.0, 5.0 / 6.0, 5.0 / 6.0, 1.0 / 6.0]
    barycentric = []
    for j in range(4):
        product = 1.0
        for k in range(4):
            if k != j:
                product = product * (points[j] - points[k])
        barycentric.append(1.0 / product)
    deriv_matrix = [[0.0] * 4 for i in range(4)]
    for i in range(4):
        for j in range(4):
            if j != i:
                deriv_matrix[i][j] = barycentric[j] / barycentric[i] / (points[i] - points[j])
        deriv_matrix[i][i] = -sum((deriv_matrix[i][j] for j in range(4) if j != i))
    norms_discrete = [2.0, 2.0 / 3.0, 2.0 / 5.0, 2.0 / 3.0]
    modal_matrix = [[weights[i] * legendre_values(points[i])[k] / norms_discrete[k] for i in range(4)] for k in range(4)]
    return (deriv_matrix, modal_matrix)

def node_slices(f, along):
    return [lax.slice_in_dim(f, j, f.shape[along], 4, along) for j in range(4)]

def first_slice(f, along):
    return lax.slice_in_dim(f, 0, 1, 1, along)

def last_slice(f, along):
    return lax.slice_in_dim(f, f.shape[along] - 1, f.shape[along], 1, along)

def alternate(pieces, along, full_shape):
    return jnp.stack(pieces, axis=along + 1).reshape(full_shape)

def combine(node_list, matrix, i):
    summed = matrix[i][0] * node_list[0]
    for j in range(1, 4):
        summed = summed + matrix[i][j] * node_list[j]
    return summed

def edge_value(node_list, i, star, matrix):
    value = combine(node_list, matrix, i)
    if i == 0:
        return value - END_PENALTY * (star - node_list[0])
    return value + END_PENALTY * (star - node_list[3])

def derivative(f, along, star_lower, star_upper, matrix):
    node_list = node_slices(f, along)
    pieces = [edge_value(node_list, 0, star_lower, matrix), combine(node_list, matrix, 1), combine(node_list, matrix, 2), edge_value(node_list, 3, star_upper, matrix)]
    return alternate(pieces, along, f.shape)

def transform(f, matrix, along):
    node_list = node_slices(f, along)
    return alternate([combine(node_list, matrix, i) for i in range(4)], along, f.shape)

def partners(lower_side, upper_side, along, lower_ghost, upper_ghost):
    count = lower_side.shape[along]
    below = jnp.concatenate([lower_ghost, lax.slice_in_dim(upper_side, 0, count - 1, 1, along)], axis=along)
    above = jnp.concatenate([lax.slice_in_dim(lower_side, 1, count, 1, along), upper_ghost], axis=along)
    return (below, above)

def euler_flux(u, d):
    density = u[0]
    velocity = u[1 + d] / density
    pressure = GAMMA_MINUS * (u[4] - 0.5 * (u[1] * u[1] + u[2] * u[2] + u[3] * u[3]) / density)
    components = [u[1 + d], u[1] * velocity, u[2] * velocity, u[3] * velocity, (u[4] + pressure) * velocity]
    components[1 + d] = components[1 + d] + pressure
    return jnp.stack(components)

def tangent_flux(u, t, d):
    return jax.vmap(lambda column: jax.jvp(lambda state: euler_flux(state, d), (u,), (column,))[1])(t)

def wave_speed(u, d):
    density = u[0]
    pressure = GAMMA_MINUS * (u[4] - 0.5 * (u[1] * u[1] + u[2] * u[2] + u[3] * u[3]) / density)
    return jnp.abs(u[1 + d] / density) + jnp.sqrt(1.4 * pressure / density)

def viscosity(base_state, shock_flags, modal_matrix):
    modal_coefs = base_state[0]
    for along in range(3):
        modal_coefs = transform(modal_coefs, modal_matrix, along)
    blocked = modal_coefs.reshape(modal_coefs.shape[0] // 4, 4, modal_coefs.shape[1] // 4, 4, modal_coefs.shape[2] // 4, 4)
    squares = blocked * blocked
    top_mask = np.ones((4, 4, 4), np.float32)
    top_mask[:3, :3, :3] = 0.0
    top_mask = jnp.asarray(top_mask, jnp.float32).reshape(1, 4, 1, 4, 1, 4)
    total_energy = lax.optimization_barrier(jnp.sum(squares, axis=(1, 3, 5)))
    top_energy = lax.optimization_barrier(jnp.sum(squares * top_mask, axis=(1, 3, 5)))
    sensor = jnp.log10(top_energy / total_energy + 1e-10)
    return EPS_TOP * shock_flags.astype(jnp.float32) * jax.nn.sigmoid((sensor - SENSOR_MID) / SENSOR_WIDTH)

def spread_nodes(per_element):
    return jnp.repeat(jnp.repeat(jnp.repeat(per_element, 4, axis=0), 4, axis=1), 4, axis=2)

def outside(lower_side, upper_side, along, d):
    if d == 2:
        return (last_slice(upper_side, along), first_slice(lower_side, along))
    return (first_slice(lower_side, along), last_slice(upper_side, along))

def residual_global(tangent, base_state, coef_nodes, matrix):
    summed = jnp.zeros_like(tangent)
    for d in range(3):
        along = 2 + d
        base_along = 1 + d
        base_nodes = node_slices(base_state, base_along)
        base_lower, base_upper = (base_nodes[0], base_nodes[3])
        ghost_lower, ghost_upper = outside(base_lower, base_upper, base_along, d)
        base_below, base_above = partners(base_lower, base_upper, base_along, ghost_lower, ghost_upper)
        speed_lower = jnp.maximum(wave_speed(base_lower, d), wave_speed(base_below, d))
        speed_upper = jnp.maximum(wave_speed(base_upper, d), wave_speed(base_above, d))
        tan_nodes = node_slices(tangent, along)
        tan_lower, tan_upper = (tan_nodes[0], tan_nodes[3])
        ghost_lower, ghost_upper = outside(tan_lower, tan_upper, along, d)
        tan_below, tan_above = partners(tan_lower, tan_upper, along, ghost_lower, ghost_upper)
        flux = tangent_flux(base_state, tangent, d)
        flux_nodes = node_slices(flux, along)
        flux_below = tangent_flux(base_below, tan_below, d)
        flux_above = tangent_flux(base_above, tan_above, d)
        star_lower = 0.5 * (flux_below + flux_nodes[0]) - 0.5 * speed_lower * (tan_lower - tan_below)
        star_upper = 0.5 * (flux_nodes[3] + flux_above) - 0.5 * speed_upper * (tan_above - tan_upper)
        mean_lower = 0.5 * (tan_lower + tan_below)
        mean_upper = 0.5 * (tan_upper + tan_above)
        lifted = coef_nodes * derivative(tangent, along, mean_lower, mean_upper, matrix)
        lift_nodes = node_slices(lifted, along)
        ghost_lower, ghost_upper = outside(lift_nodes[0], lift_nodes[3], along, d)
        lift_below, lift_above = partners(lift_nodes[0], lift_nodes[3], along, ghost_lower, ghost_upper)
        visc_lower = 0.5 * (lift_nodes[0] + lift_below)
        visc_upper = 0.5 * (lift_nodes[3] + lift_above)
        summed = summed + (derivative(lifted, along, visc_lower, visc_upper, matrix) - derivative(flux, along, star_lower, star_upper, matrix))
    return summed

def reference(tangent, base_state, shock_flags):
    deriv_matrix, modal_matrix = node_tables()
    coef_nodes = spread_nodes(viscosity(base_state, shock_flags, modal_matrix))

    def one_column(column):
        start = column[None]
        section_one = start + STEP * residual_global(start, base_state, coef_nodes, deriv_matrix)
        final = 0.5 * start + 0.5 * (section_one + STEP * residual_global(section_one, base_state, coef_nodes, deriv_matrix))
        return final[0]
    return lax.map(one_column, tangent)
```

```python
import math

import jax
import jax.numpy as jnp
import numpy as np
from jax import lax
from jax.experimental import pallas as pl
from jax.experimental.pallas import tpu as pltpu
from jax.sharding import PartitionSpec as P

STEP = 0.1
COLS = 8
LANES = 128
V1, V2, V3, W1, W2, W3, KE, HH, SX, SY, SZ, NU = range(12)
FACE = 160
FACE_NAMES = (V1, V2, V3, KE, HH, NU)
COEF_ROWS = 32


def node_tables():
    inner_point = math.sqrt(0.2)
    points = [-1.0, -inner_point, inner_point, 1.0]
    weights = [1.0 / 6.0, 5.0 / 6.0, 5.0 / 6.0, 1.0 / 6.0]
    barycentric = []
    for j in range(4):
        product = 1.0
        for k in range(4):
            if k != j:
                product = product * (points[j] - points[k])
        barycentric.append(1.0 / product)
    deriv = [[0.0] * 4 for i in range(4)]
    for i in range(4):
        for j in range(4):
            if j != i:
                deriv[i][j] = barycentric[j] / barycentric[i] / (points[i] - points[j])
        deriv[i][i] = -sum((deriv[i][j] for j in range(4) if j != i))
    norms = [2.0, 2.0 / 3.0, 2.0 / 5.0, 2.0 / 3.0]
    legendre = [
        lambda x: 1.0,
        lambda x: x,
        lambda x: 0.5 * (3.0 * x * x - 1.0),
        lambda x: 0.5 * (5.0 * x * x * x - 3.0 * x),
    ]
    modal = [[weights[i] * legendre[k](points[i]) / norms[k] for i in range(4)] for k in range(4)]
    return deriv, modal


DERIV, MODAL = node_tables()


def span_table():
    m = np.zeros((LANES, LANES), np.float64)
    for e in range(LANES // 4):
        for i in range(4):
            for j in range(4):
                if i != j:
                    m[4 * e + j, 4 * e + i] = DERIV[i][j]
        m[4 * e, 4 * e] = DERIV[0][0] + 3.0
        m[4 * e + 3, 4 * e + 3] = DERIV[3][3] - 3.0
        m[(4 * e + 4) % LANES, 4 * e + 3] += 3.0
        m[(4 * e - 1) % LANES, 4 * e] -= 3.0
    m = m.astype(np.float32)
    hi = m.astype(jnp.bfloat16)
    lo = (m - hi.astype(np.float32)).astype(jnp.bfloat16)
    zero = np.zeros_like(lo)
    return np.block([[hi, lo], [hi, zero]])


def row(f, x, y):
    return (f * 16 + x * 4 + y) * COLS


def face_row(f, n):
    return (f * 4 + n) * COLS


def tan_in(ref, f, x, y):
    return ref[pl.ds(f * 16 + x * 4 + y, COLS, stride=80), :]


def coef(ref, name, x, y):
    r = name * 16 + x * 4 + y
    return ref[r : r + 1, :]


def group_transform(f, matrix, axis, index, step):
    size = f.shape[axis]
    total = None
    for offset in range(-3, 4):
        c = jnp.zeros_like(f)
        for i in range(4):
            if 0 <= i + offset < 4:
                c = jnp.where(index == i, matrix[i][i + offset], c)
        moved = f if offset == 0 else pltpu.roll(f, (-offset * step) % size, axis)
        term = c * moved
        total = term if total is None else total + term
    return total


def base_coefs(base_ref, flags_ref, coef_ref):
    u = [base_ref[f * 16 : (f + 1) * 16, :] for f in range(5)]
    inv = 1.0 / u[0]
    v = [u[1 + d] * inv for d in range(3)]
    ke = 0.5 * (v[0] * v[0] + v[1] * v[1] + v[2] * v[2])
    pressure = 0.4 * (u[4] - ke * u[0])
    sound = jnp.sqrt(1.4 * pressure * inv)
    speed = [jnp.abs(v[d]) + sound for d in range(3)]
    lane = lax.broadcasted_iota(jnp.int32, (16, LANES), 1)
    sub = lax.broadcasted_iota(jnp.int32, (16, LANES), 0)
    zi, yi, xi = lane % 4, sub % 4, sub // 4
    near = jnp.where(
        zi == 3, pltpu.roll(speed[2], LANES - 1, 1), pltpu.roll(speed[2], 1, 1)
    )
    sz = jnp.where((zi == 0) | (zi == 3), 3.0 * jnp.maximum(speed[2], near), 0.0)
    modal = group_transform(u[0], MODAL, 1, zi, 1)
    modal = group_transform(modal, MODAL, 0, yi, 1)
    modal = group_transform(modal, MODAL, 0, xi, 4)
    squares = modal * modal
    edge = jnp.where((zi == 3) | (yi == 3) | (xi == 3), squares, 0.0)
    ones = [[1.0] * 4] * 4
    sums = []
    for s in (squares, edge):
        s = jnp.broadcast_to(jnp.sum(s, axis=0, keepdims=True), (8, LANES))
        sums.append(group_transform(s, ones, 1, zi[:8], 1))
    sensor = jnp.log(sums[1] / sums[0] + 1e-10) * (1.0 / math.log(10.0))
    shape = 1.0 / (1.0 + jnp.exp(-(sensor + 2.3) * 2.0))
    spread = jnp.where(
        lax.broadcasted_iota(jnp.int32, (32, LANES), 1) // 4
        == lax.broadcasted_iota(jnp.int32, (32, LANES), 0),
        1.0,
        0.0,
    )
    flags = jnp.broadcast_to(flags_ref[...].astype(jnp.float32), (8, 32))
    flags = jnp.dot(flags, spread, preferred_element_type=jnp.float32)
    nu = 0.1 * flags * shape
    nu = jnp.concatenate([nu, nu], axis=0)
    table = {
        V1: v[0], V2: v[1], V3: v[2],
        W1: 0.4 * v[0], W2: 0.4 * v[1], W3: 0.4 * v[2],
        KE: 0.4 * ke, HH: (u[4] + pressure) * inv,
        SX: speed[0], SY: speed[1], SZ: sz, NU: nu,
    }
    for name, value in table.items():
        coef_ref[name * 16 : (name + 1) * 16, :] = value


def pack_faces(load, outs, odd_x, odd_y):
    for axis, (near, far), odd in ((0, outs[:2], odd_x), (1, outs[2:], odd_y)):
        for f in range(5):
            for n in range(4):
                line = [load(f, k, n) if axis == 0 else load(f, n, k) for k in range(4)]
                lower = line[0] * DERIV[0][0]
                upper = line[3] * DERIV[3][3]
                for k in range(1, 4):
                    lower = lower + DERIV[0][k] * line[k]
                    upper = upper + DERIV[3][3 - k] * line[3 - k]
                r = face_row(f, n)
                near[r : r + 8, :] = jnp.where(odd, line[0], line[3])
                far[r : r + 8, :] = jnp.where(odd, line[3], line[0])
                near[FACE + r : FACE + r + 8, :] = jnp.where(odd, lower, upper)
                far[FACE + r : FACE + r + 8, :] = jnp.where(odd, upper, lower)


def pack_kernel(t_ref, base_ref, flags_ref, coef_ref, xn, xf, yn, yf):
    odd_x = lax.axis_index("gx") % 2 == 1
    odd_y = lax.axis_index("gy") % 2 == 1
    base_coefs(base_ref, flags_ref, coef_ref)
    pack_faces(lambda f, x, y: tan_in(t_ref, f, x, y), (xn, xf, yn, yf), odd_x, odd_y)
    for axis, (near, far), odd in ((0, (xn, xf), odd_x), (1, (yn, yf), odd_y)):
        for place, name in enumerate(FACE_NAMES + (SX + axis,)):
            first = name * 16
            if axis == 0:
                lower = coef_ref[first : first + 4, :]
                upper = coef_ref[first + 12 : first + 16, :]
            else:
                lower = coef_ref[pl.ds(first, 4, stride=4), :]
                upper = coef_ref[pl.ds(first + 3, 4, stride=4), :]
            r = 2 * FACE + 4 * place
            near[r : r + 4, :] = jnp.where(odd, lower, upper)
            far[r : r + 4, :] = jnp.where(odd, upper, lower)
        r = 2 * FACE + 28
        near[r : r + 4, :] = jnp.zeros((4, LANES), jnp.float32)
        far[r : r + 4, :] = jnp.zeros((4, LANES), jnp.float32)


def flux(d, t, v, dp, e, hh):
    u = t[1 + d] - v[d] * t[0]
    out = [t[1 + d]]
    for i in range(3):
        value = v[d] * t[1 + i] + v[i] * u
        out.append(value + dp if i == d else value)
    out.append(v[d] * e + hh * u)
    return out


def section(load, coef_ref, recv, coef_recv, odd_x, odd_y, wm_ref, acc, ops, aux, finish):
    nodes = [(x, y) for x in range(4) for y in range(4)]
    zi = lax.broadcasted_iota(jnp.int32, (COLS, LANES), 1) % 4
    top_lane = zi == 3

    def split(r, value):
        hi = value.astype(jnp.bfloat16)
        lo = (value - hi.astype(jnp.float32)).astype(jnp.bfloat16)
        return hi, lo

    def put(f, x, y, pair):
        r = row(f, x, y)
        ops[r : r + 16, :LANES] = pair[0]
        ops[r : r + 16, LANES:] = pair[1]

    for x in range(4):
        for f in range(5):
            for y in (0, 2):
                value = jnp.concatenate([load(f, x, y), load(f, x, y + 1)], axis=0)
                put(f, x, y, split(0, value))
    chunk = 128
    for c in range(640 // chunk):
        both = jnp.dot(
            ops[c * chunk : (c + 1) * chunk, :], wm_ref[...], preferred_element_type=jnp.float32
        )
        acc[c * chunk : (c + 1) * chunk, :] = both[:, :LANES] + both[:, LANES:]

    for x in range(4):
        for y in (0, 2):
            parts = []
            for yy in (y, y + 1):
                t = [load(f, x, yy) for f in range(5)]
                v = [coef(coef_ref, V1 + d, x, yy) for d in range(3)]
                w = [coef(coef_ref, W1 + d, x, yy) for d in range(3)]
                dp = 0.4 * t[4] + coef(coef_ref, KE, x, yy) * t[0]
                for d in range(3):
                    dp = dp - w[d] * t[1 + d]
                e = t[4] + dp
                k = (x * 4 + yy) * 16
                aux[k : k + 8, :] = dp
                aux[k + 8 : k + 16, :] = e
                g = flux(2, t, v, dp, e, coef(coef_ref, HH, x, yy))
                nu = coef(coef_ref, NU, x, yy)
                out = []
                for f in range(5):
                    r = row(f, x, yy)
                    out.append(nu * acc[r : r + 8, :] - g[f])
                parts.append(out)
            for f in range(5):
                value = jnp.concatenate([parts[0][f], parts[1][f]], axis=0)
                put(f, x, y, split(0, value))
    for c in range(640 // chunk):
        both = jnp.dot(
            ops[c * chunk : (c + 1) * chunk, :], wm_ref[...], preferred_element_type=jnp.float32
        )
        acc[c * chunk : (c + 1) * chunk, :] = both[:, :LANES] + both[:, LANES:]

    for axis, odd in ((0, odd_x), (1, odd_y)):
        near, far = recv[2 * axis : 2 * axis + 2]
        (near_c, near_at), (far_c, far_at) = coef_recv[2 * axis : 2 * axis + 2]

        def pick(low, r, rows=8):
            a, b = near[r : r + rows, :], far[r : r + rows, :]
            return jnp.where(odd, a, b) if low else jnp.where(odd, b, a)

        def pick_coef(low, place, n):
            r = 4 * place + n
            a = near_c[near_at + r : near_at + r + 1, :]
            b = far_c[far_at + r : far_at + r + 1, :]
            return jnp.where(odd, a, b) if low else jnp.where(odd, b, a)

        for n in range(4):
            line = [(k, n) if axis == 0 else (n, k) for k in range(4)]
            t = [[load(f, x, y) for f in range(5)] for x, y in line]
            g = []
            for k, (x, y) in enumerate(line):
                v = [coef(coef_ref, V1 + d, x, y) for d in range(3)]
                r = (x * 4 + y) * 16
                g.append(
                    flux(axis, t[k], v, aux[r : r + 8, :], aux[r + 8 : r + 16, :],
                         coef(coef_ref, HH, x, y))
                )
            nu = coef(coef_ref, NU, *line[0])
            sides = []
            for low in (True, False):
                mine = t[0] if low else t[3]
                far_t = [pick(low, face_row(f, n)) for f in range(5)]
                v = [pick_coef(low, d, n) for d in range(3)]
                dp = 0.4 * far_t[4] + pick_coef(low, 3, n) * far_t[0]
                for d in range(3):
                    dp = dp - (0.4 * v[d]) * far_t[1 + d]
                far_g = flux(axis, far_t, v, dp, far_t[4] + dp, pick_coef(low, 4, n))
                far_nu = pick_coef(low, 5, n)
                own_s = coef(coef_ref, SX + axis, *(line[0] if low else line[3]))
                s3 = 3.0 * jnp.maximum(own_s, pick_coef(low, 6, n))
                far_f, jump, mean = [], [], []
                for f in range(5):
                    step3 = 3.0 * (far_t[f] - mine[f])
                    far_d = pick(low, FACE + face_row(f, n))
                    far_q = far_d - step3 if low else far_d + step3
                    value = 3.0 * (far_nu * far_q - far_g[f])
                    far_f.append(-value if low else value)
                    jump.append(s3 * (far_t[f] - mine[f]))
                    mean.append(3.0 * far_t[f])
                sides.append((far_f, jump, mean))
            for f in range(5):
                tt = [t[k][f] for k in range(4)]
                fl = []
                for i in range(4):
                    q = None
                    for k in range(4):
                        if k != i:
                            term = DERIV[i][k] * tt[k]
                            q = term if q is None else q + term
                    if i == 0:
                        q = q - sides[0][2][f]
                    if i == 3:
                        q = q + sides[1][2][f]
                    fl.append(nu * q - g[i][f])
                for i, (x, y) in enumerate(line):
                    total = None
                    for k in range(4):
                        if k != i:
                            term = DERIV[i][k] * fl[k]
                            total = term if total is None else total + term
                    if i == 0:
                        total = total + (sides[0][0][f] + sides[0][1][f])
                    if i == 3:
                        total = total + (sides[1][0][f] + sides[1][1][f])
                    r = row(f, x, y)
                    total = total + acc[r : r + 8, :]
                    if axis == 0:
                        tz = tt[i]
                        other = jnp.where(
                            top_lane, pltpu.roll(tz, LANES - 1, 1), pltpu.roll(tz, 1, 1)
                        )
                        total = total + coef(coef_ref, SZ, x, y) * (other - tz)
                        acc[r : r + 8, :] = total
                    else:
                        finish(f, x, y, tt[i], total)


def first_kernel(
    t_ref, coef_ref, wm_ref, rxn, rxf, ryn, ryf, s_ref, xn, xf, yn, yf, acc, ops, aux
):
    odd_x = lax.axis_index("gx") % 2 == 1
    odd_y = lax.axis_index("gy") % 2 == 1

    def finish(f, x, y, t, total):
        r = row(f, x, y)
        s_ref[r : r + 8, :] = t + STEP * total

    faces = (rxn, rxf, ryn, ryf)
    section(
        lambda f, x, y: tan_in(t_ref, f, x, y), coef_ref, faces,
        [(ref, 2 * FACE) for ref in faces], odd_x, odd_y, wm_ref, acc, ops, aux, finish,
    )

    def load(f, x, y):
        r = row(f, x, y)
        return s_ref[r : r + 8, :]

    pack_faces(load, (xn, xf, yn, yf), odd_x, odd_y)


def second_kernel(
    t_ref, s_ref, coef_ref, wm_ref, cxn, cxf, cyn, cyf, rxn, rxf, ryn, ryf, out_ref, acc, ops, aux
):
    odd_x = lax.axis_index("gx") % 2 == 1
    odd_y = lax.axis_index("gy") % 2 == 1

    def load(f, x, y):
        r = row(f, x, y)
        return s_ref[r : r + 8, :]

    def finish(f, x, y, s, total):
        value = 0.5 * tan_in(t_ref, f, x, y) + (0.5 * s + (0.5 * STEP) * total)
        out_ref[pl.ds(f * 16 + x * 4 + y, COLS, stride=80), :] = value

    section(
        load, coef_ref, (rxn, rxf, ryn, ryf),
        [(ref, 2 * FACE) for ref in (cxn, cxf, cyn, cyf)],
        odd_x, odd_y, wm_ref, acc, ops, aux, finish,
    )


def call(kernel, shapes, scratch, args, cost):
    vmem = pl.BlockSpec(memory_space=pltpu.VMEM)
    return pl.pallas_call(
        kernel,
        out_shape=[jax.ShapeDtypeStruct(s, jnp.float32) for s in shapes],
        in_specs=[vmem] * len(args),
        out_specs=[vmem] * len(shapes),
        scratch_shapes=scratch,
        compiler_params=pltpu.CompilerParams(vmem_limit_bytes=32 * 1024 * 1024),
        cost_estimate=pl.CostEstimate(flops=cost, bytes_accessed=1000000, transcendentals=0),
    )(*args)


def exchange(messages):
    size_x, size_y = lax.axis_size("gx"), lax.axis_size("gy")

    def pairs(size, first):
        out = []
        for i in range(first, size - 1, 2):
            out += [(i, i + 1), (i + 1, i)]
        if first == 1:
            out += [(0, 0)]
            if size % 2 == 0:
                out += [(size - 1, size - 1)]
        return out

    xn, xf, yn, yf = messages
    got_xn = lax.ppermute(xn, "gx", pairs(size_x, 0))
    got_yn = lax.ppermute(yn, "gy", pairs(size_y, 0))
    got_xf = lax.ppermute(xf, "gx", pairs(size_x, 1))
    got_yf = lax.ppermute(yf, "gy", pairs(size_y, 1))
    return got_xn, got_xf, got_yn, got_yf


def per_device(tangent, base_state, shock_flags):
    t = tangent.reshape(640, LANES)
    base = base_state.reshape(80, LANES)
    flags = shock_flags.reshape(1, 32)
    wm = jnp.asarray(span_table())
    message = (2 * FACE + COEF_ROWS, LANES)
    short = (2 * FACE, LANES)
    scratch = [
        pltpu.VMEM((640, LANES), jnp.float32),
        pltpu.VMEM((640, 2 * LANES), jnp.bfloat16),
        pltpu.VMEM((256, LANES), jnp.float32),
    ]
    coefs, *faces = call(
        pack_kernel, [(192, LANES)] + [message] * 4, [], [t, base, flags], 1000000
    )
    got = exchange(faces)
    s, *faces = call(
        first_kernel, [(640, LANES)] + [short] * 4, scratch, [t, coefs, wm, *got], 10000000
    )
    again = exchange(faces)
    (out,) = call(
        second_kernel, [(640, LANES)], scratch, [t, s, coefs, wm, *got, *again], 10000000
    )
    return out.reshape(tangent.shape)


def solution(mesh):
    in_specs = (P(None, None, "gx", "gy", None), P(None, "gx", "gy", None), P("gx", "gy", None))
    out_specs = P(None, None, "gx", "gy", None)
    return jax.shard_map(
        per_device, mesh=mesh, in_specs=in_specs, out_specs=out_specs, check_vma=False
    )
```

```python
import math

import jax
import jax.numpy as jnp
import numpy as np
from jax import lax
from jax.experimental import pallas as pl
from jax.experimental.pallas import tpu as pltpu
from jax.sharding import PartitionSpec as P

STEP = 0.1
COLS = 8
LANES = 128
V1, V2, V3, W1, W2, W3, KE, HH, SX, SY, SZ, NU = range(12)
FACE = 160
FACE_NAMES = (V1, V2, V3, KE, HH, NU)
COEF_ROWS = 32
ORDER = (1, 3, 0, 2)


def node_tables():
    inner_point = math.sqrt(0.2)
    points = [-1.0, -inner_point, inner_point, 1.0]
    weights = [1.0 / 6.0, 5.0 / 6.0, 5.0 / 6.0, 1.0 / 6.0]
    barycentric = []
    for j in range(4):
        product = 1.0
        for k in range(4):
            if k != j:
                product = product * (points[j] - points[k])
        barycentric.append(1.0 / product)
    deriv = [[0.0] * 4 for i in range(4)]
    for i in range(4):
        for j in range(4):
            if j != i:
                deriv[i][j] = barycentric[j] / barycentric[i] / (points[i] - points[j])
        deriv[i][i] = -sum((deriv[i][j] for j in range(4) if j != i))
    norms = [2.0, 2.0 / 3.0, 2.0 / 5.0, 2.0 / 3.0]
    legendre = [
        lambda x: 1.0,
        lambda x: x,
        lambda x: 0.5 * (3.0 * x * x - 1.0),
        lambda x: 0.5 * (5.0 * x * x * x - 3.0 * x),
    ]
    modal = [[weights[i] * legendre[k](points[i]) / norms[k] for i in range(4)] for k in range(4)]
    return deriv, modal


DERIV, MODAL = node_tables()


def span_table():
    m = np.zeros((LANES, LANES), np.float64)
    for e in range(LANES // 4):
        for i in range(4):
            for j in range(4):
                if i != j:
                    m[4 * e + j, 4 * e + i] = DERIV[i][j]
        m[4 * e, 4 * e] = DERIV[0][0] + 3.0
        m[4 * e + 3, 4 * e + 3] = DERIV[3][3] - 3.0
        m[(4 * e + 4) % LANES, 4 * e + 3] += 3.0
        m[(4 * e - 1) % LANES, 4 * e] -= 3.0
    m = m.astype(np.float32)
    hi = m.astype(jnp.bfloat16)
    lo = (m - hi.astype(np.float32)).astype(jnp.bfloat16)
    zero = np.zeros_like(lo)
    return np.block([[hi, lo], [hi, zero]])


def row(f, x, y):
    return (f * 16 + x * 4 + y) * COLS


def face_row(f, n):
    return (f * 4 + n) * COLS


def tan_in(ref, f, x, y):
    return ref[pl.ds(f * 16 + x * 4 + y, COLS, stride=80), :]


def coef(ref, name, x, y):
    r = name * 16 + x * 4 + y
    return ref[r : r + 1, :]


def group_transform(f, matrix, axis, index, step):
    size = f.shape[axis]
    total = None
    for offset in range(-3, 4):
        c = jnp.zeros_like(f)
        for i in range(4):
            if 0 <= i + offset < 4:
                c = jnp.where(index == i, matrix[i][i + offset], c)
        moved = f if offset == 0 else pltpu.roll(f, (-offset * step) % size, axis)
        term = c * moved
        total = term if total is None else total + term
    return total


def base_coefs(base_ref, flags_ref, coef_ref):
    u = [base_ref[f * 16 : (f + 1) * 16, :] for f in range(5)]
    inv = 1.0 / u[0]
    v = [u[1 + d] * inv for d in range(3)]
    ke = 0.5 * (v[0] * v[0] + v[1] * v[1] + v[2] * v[2])
    pressure = 0.4 * (u[4] - ke * u[0])
    sound = jnp.sqrt(1.4 * pressure * inv)
    speed = [jnp.abs(v[d]) + sound for d in range(3)]
    lane = lax.broadcasted_iota(jnp.int32, (16, LANES), 1)
    sub = lax.broadcasted_iota(jnp.int32, (16, LANES), 0)
    zi, yi, xi = lane % 4, sub % 4, sub // 4
    near = jnp.where(
        zi == 3, pltpu.roll(speed[2], LANES - 1, 1), pltpu.roll(speed[2], 1, 1)
    )
    sz = jnp.where((zi == 0) | (zi == 3), 3.0 * jnp.maximum(speed[2], near), 0.0)
    modal = group_transform(u[0], MODAL, 1, zi, 1)
    modal = group_transform(modal, MODAL, 0, yi, 1)
    modal = group_transform(modal, MODAL, 0, xi, 4)
    squares = modal * modal
    edge = jnp.where((zi == 3) | (yi == 3) | (xi == 3), squares, 0.0)
    ones = [[1.0] * 4] * 4
    sums = []
    for s in (squares, edge):
        s = jnp.broadcast_to(jnp.sum(s, axis=0, keepdims=True), (8, LANES))
        sums.append(group_transform(s, ones, 1, zi[:8], 1))
    sensor = jnp.log(sums[1] / sums[0] + 1e-10) * (1.0 / math.log(10.0))
    shape = 1.0 / (1.0 + jnp.exp(-(sensor + 2.3) * 2.0))
    spread = jnp.where(
        lax.broadcasted_iota(jnp.int32, (32, LANES), 1) // 4
        == lax.broadcasted_iota(jnp.int32, (32, LANES), 0),
        1.0,
        0.0,
    )
    flags = jnp.broadcast_to(flags_ref[...].astype(jnp.float32), (8, 32))
    flags = jnp.dot(flags, spread, preferred_element_type=jnp.float32)
    nu = 0.1 * flags * shape
    nu = jnp.concatenate([nu, nu], axis=0)
    table = {
        V1: v[0], V2: v[1], V3: v[2],
        W1: 0.4 * v[0], W2: 0.4 * v[1], W3: 0.4 * v[2],
        KE: 0.4 * ke, HH: (u[4] + pressure) * inv,
        SX: speed[0], SY: speed[1], SZ: sz, NU: nu,
    }
    for name, value in table.items():
        coef_ref[name * 16 : (name + 1) * 16, :] = value


def pack_faces(load, outs, odd_x, odd_y):
    for axis, (near, far), odd in ((0, outs[:2], odd_x), (1, outs[2:], odd_y)):
        for f in range(5):
            for n in range(4):
                line = [load(f, k, n) if axis == 0 else load(f, n, k) for k in range(4)]
                lower = line[0] * DERIV[0][0]
                upper = line[3] * DERIV[3][3]
                for k in range(1, 4):
                    lower = lower + DERIV[0][k] * line[k]
                    upper = upper + DERIV[3][3 - k] * line[3 - k]
                r = face_row(f, n)
                near[r : r + 8, :] = jnp.where(odd, line[0], line[3])
                far[r : r + 8, :] = jnp.where(odd, line[3], line[0])
                near[FACE + r : FACE + r + 8, :] = jnp.where(odd, lower, upper)
                far[FACE + r : FACE + r + 8, :] = jnp.where(odd, upper, lower)


def by_face(refs):
    return tuple(refs[ORDER.index(face)] for face in range(4))


def pack_kernel(t_ref, base_ref, flags_ref, coef_ref, *sent):
    xn, xf, yn, yf = by_face(sent)
    odd_x = lax.axis_index("gx") % 2 == 1
    odd_y = lax.axis_index("gy") % 2 == 1
    base_coefs(base_ref, flags_ref, coef_ref)
    pack_faces(lambda f, x, y: tan_in(t_ref, f, x, y), (xn, xf, yn, yf), odd_x, odd_y)
    for axis, (near, far), odd in ((0, (xn, xf), odd_x), (1, (yn, yf), odd_y)):
        for place, name in enumerate(FACE_NAMES + (SX + axis,)):
            first = name * 16
            if axis == 0:
                lower = coef_ref[first : first + 4, :]
                upper = coef_ref[first + 12 : first + 16, :]
            else:
                lower = coef_ref[pl.ds(first, 4, stride=4), :]
                upper = coef_ref[pl.ds(first + 3, 4, stride=4), :]
            r = 2 * FACE + 4 * place
            near[r : r + 4, :] = jnp.where(odd, lower, upper)
            far[r : r + 4, :] = jnp.where(odd, upper, lower)
        r = 2 * FACE + 28
        near[r : r + 4, :] = jnp.zeros((4, LANES), jnp.float32)
        far[r : r + 4, :] = jnp.zeros((4, LANES), jnp.float32)


def flux(d, t, v, dp, e, hh):
    u = t[1 + d] - v[d] * t[0]
    out = [t[1 + d]]
    for i in range(3):
        value = v[d] * t[1 + i] + v[i] * u
        out.append(value + dp if i == d else value)
    out.append(v[d] * e + hh * u)
    return out


def section(load, coef_ref, recv, coef_recv, odd_x, odd_y, wm_ref, acc, ops, aux, finish):
    nodes = [(x, y) for x in range(4) for y in range(4)]
    zi = lax.broadcasted_iota(jnp.int32, (COLS, LANES), 1) % 4
    top_lane = zi == 3

    def split(r, value):
        hi = value.astype(jnp.bfloat16)
        lo = (value - hi.astype(jnp.float32)).astype(jnp.bfloat16)
        return hi, lo

    def put(f, x, y, pair):
        r = row(f, x, y)
        ops[r : r + 16, :LANES] = pair[0]
        ops[r : r + 16, LANES:] = pair[1]

    for x in range(4):
        for f in range(5):
            for y in (0, 2):
                value = jnp.concatenate([load(f, x, y), load(f, x, y + 1)], axis=0)
                put(f, x, y, split(0, value))
    chunk = 128
    for c in range(640 // chunk):
        both = jnp.dot(
            ops[c * chunk : (c + 1) * chunk, :], wm_ref[...], preferred_element_type=jnp.float32
        )
        acc[c * chunk : (c + 1) * chunk, :] = both[:, :LANES] + both[:, LANES:]

    for x in range(4):
        for y in (0, 2):
            parts = []
            for yy in (y, y + 1):
                t = [load(f, x, yy) for f in range(5)]
                v = [coef(coef_ref, V1 + d, x, yy) for d in range(3)]
                w = [coef(coef_ref, W1 + d, x, yy) for d in range(3)]
                dp = 0.4 * t[4] + coef(coef_ref, KE, x, yy) * t[0]
                for d in range(3):
                    dp = dp - w[d] * t[1 + d]
                e = t[4] + dp
                k = (x * 4 + yy) * 16
                aux[k : k + 8, :] = dp
                aux[k + 8 : k + 16, :] = e
                g = flux(2, t, v, dp, e, coef(coef_ref, HH, x, yy))
                nu = coef(coef_ref, NU, x, yy)
                out = []
                for f in range(5):
                    r = row(f, x, yy)
                    out.append(nu * acc[r : r + 8, :] - g[f])
                parts.append(out)
            for f in range(5):
                value = jnp.concatenate([parts[0][f], parts[1][f]], axis=0)
                put(f, x, y, split(0, value))
    for c in range(640 // chunk):
        both = jnp.dot(
            ops[c * chunk : (c + 1) * chunk, :], wm_ref[...], preferred_element_type=jnp.float32
        )
        acc[c * chunk : (c + 1) * chunk, :] = both[:, :LANES] + both[:, LANES:]

    for axis, odd in ((0, odd_x), (1, odd_y)):
        near, far = recv[2 * axis : 2 * axis + 2]
        (near_c, near_at), (far_c, far_at) = coef_recv[2 * axis : 2 * axis + 2]

        def pick(low, r, rows=8):
            a, b = near[r : r + rows, :], far[r : r + rows, :]
            return jnp.where(odd, a, b) if low else jnp.where(odd, b, a)

        def pick_coef(low, place, n):
            r = 4 * place + n
            a = near_c[near_at + r : near_at + r + 1, :]
            b = far_c[far_at + r : far_at + r + 1, :]
            return jnp.where(odd, a, b) if low else jnp.where(odd, b, a)

        for n in range(4):
            line = [(k, n) if axis == 0 else (n, k) for k in range(4)]
            t = [[load(f, x, y) for f in range(5)] for x, y in line]
            g = []
            for k, (x, y) in enumerate(line):
                v = [coef(coef_ref, V1 + d, x, y) for d in range(3)]
                r = (x * 4 + y) * 16
                g.append(
                    flux(axis, t[k], v, aux[r : r + 8, :], aux[r + 8 : r + 16, :],
                         coef(coef_ref, HH, x, y))
                )
            nu = coef(coef_ref, NU, *line[0])
            sides = []
            for low in (True, False):
                mine = t[0] if low else t[3]
                far_t = [pick(low, face_row(f, n)) for f in range(5)]
                v = [pick_coef(low, d, n) for d in range(3)]
                dp = 0.4 * far_t[4] + pick_coef(low, 3, n) * far_t[0]
                for d in range(3):
                    dp = dp - (0.4 * v[d]) * far_t[1 + d]
                far_g = flux(axis, far_t, v, dp, far_t[4] + dp, pick_coef(low, 4, n))
                far_nu = pick_coef(low, 5, n)
                own_s = coef(coef_ref, SX + axis, *(line[0] if low else line[3]))
                s3 = 3.0 * jnp.maximum(own_s, pick_coef(low, 6, n))
                far_f, jump, mean = [], [], []
                for f in range(5):
                    step3 = 3.0 * (far_t[f] - mine[f])
                    far_d = pick(low, FACE + face_row(f, n))
                    far_q = far_d - step3 if low else far_d + step3
                    value = 3.0 * (far_nu * far_q - far_g[f])
                    far_f.append(-value if low else value)
                    jump.append(s3 * (far_t[f] - mine[f]))
                    mean.append(3.0 * far_t[f])
                sides.append((far_f, jump, mean))
            for f in range(5):
                tt = [t[k][f] for k in range(4)]
                fl = []
                for i in range(4):
                    q = None
                    for k in range(4):
                        if k != i:
                            term = DERIV[i][k] * tt[k]
                            q = term if q is None else q + term
                    if i == 0:
                        q = q - sides[0][2][f]
                    if i == 3:
                        q = q + sides[1][2][f]
                    fl.append(nu * q - g[i][f])
                for i, (x, y) in enumerate(line):
                    total = None
                    for k in range(4):
                        if k != i:
                            term = DERIV[i][k] * fl[k]
                            total = term if total is None else total + term
                    if i == 0:
                        total = total + (sides[0][0][f] + sides[0][1][f])
                    if i == 3:
                        total = total + (sides[1][0][f] + sides[1][1][f])
                    r = row(f, x, y)
                    total = total + acc[r : r + 8, :]
                    if axis == 0:
                        tz = tt[i]
                        other = jnp.where(
                            top_lane, pltpu.roll(tz, LANES - 1, 1), pltpu.roll(tz, 1, 1)
                        )
                        total = total + coef(coef_ref, SZ, x, y) * (other - tz)
                        acc[r : r + 8, :] = total
                    else:
                        finish(f, x, y, tt[i], total)


def first_kernel(t_ref, coef_ref, wm_ref, r0, r1, r2, r3, s_ref, m0, m1, m2, m3, acc, ops, aux):
    odd_x = lax.axis_index("gx") % 2 == 1
    odd_y = lax.axis_index("gy") % 2 == 1

    def finish(f, x, y, t, total):
        r = row(f, x, y)
        s_ref[r : r + 8, :] = t + STEP * total

    faces = by_face((r0, r1, r2, r3))
    section(
        lambda f, x, y: tan_in(t_ref, f, x, y), coef_ref, faces,
        [(ref, 2 * FACE) for ref in faces], odd_x, odd_y, wm_ref, acc, ops, aux, finish,
    )

    def load(f, x, y):
        r = row(f, x, y)
        return s_ref[r : r + 8, :]

    pack_faces(load, by_face((m0, m1, m2, m3)), odd_x, odd_y)


def second_kernel(
    t_ref, s_ref, coef_ref, wm_ref, c0, c1, c2, c3, r0, r1, r2, r3, out_ref, acc, ops, aux
):
    odd_x = lax.axis_index("gx") % 2 == 1
    odd_y = lax.axis_index("gy") % 2 == 1

    def load(f, x, y):
        r = row(f, x, y)
        return s_ref[r : r + 8, :]

    def finish(f, x, y, s, total):
        value = 0.5 * tan_in(t_ref, f, x, y) + (0.5 * s + (0.5 * STEP) * total)
        out_ref[pl.ds(f * 16 + x * 4 + y, COLS, stride=80), :] = value

    section(
        load, coef_ref, by_face((r0, r1, r2, r3)),
        [(ref, 2 * FACE) for ref in by_face((c0, c1, c2, c3))],
        odd_x, odd_y, wm_ref, acc, ops, aux, finish,
    )


def call(kernel, shapes, scratch, args, cost):
    vmem = pl.BlockSpec(memory_space=pltpu.VMEM)
    return pl.pallas_call(
        kernel,
        out_shape=[jax.ShapeDtypeStruct(s, jnp.float32) for s in shapes],
        in_specs=[vmem] * len(args),
        out_specs=[vmem] * len(shapes),
        scratch_shapes=scratch,
        compiler_params=pltpu.CompilerParams(vmem_limit_bytes=32 * 1024 * 1024),
        cost_estimate=pl.CostEstimate(flops=cost, bytes_accessed=1000000, transcendentals=0),
    )(*args)


def exchange(messages):
    size_x, size_y = lax.axis_size("gx"), lax.axis_size("gy")

    def pairs(size, first):
        out = []
        for i in range(first, size - 1, 2):
            out += [(i, i + 1), (i + 1, i)]
        if first == 1:
            out += [(0, 0)]
            if size % 2 == 0:
                out += [(size - 1, size - 1)]
        return out

    plan = (
        ("gx", pairs(size_x, 0)),
        ("gx", pairs(size_x, 1)),
        ("gy", pairs(size_y, 0)),
        ("gy", pairs(size_y, 1)),
    )
    return [lax.ppermute(m, *plan[face]) for m, face in zip(messages, ORDER)]


def per_device(tangent, base_state, shock_flags):
    t = tangent.reshape(640, LANES)
    base = base_state.reshape(80, LANES)
    flags = shock_flags.reshape(1, 32)
    wm = jnp.asarray(span_table())
    message = (2 * FACE + COEF_ROWS, LANES)
    short = (2 * FACE, LANES)
    scratch = [
        pltpu.VMEM((640, LANES), jnp.float32),
        pltpu.VMEM((640, 2 * LANES), jnp.bfloat16),
        pltpu.VMEM((256, LANES), jnp.float32),
    ]
    coefs, *faces = call(
        pack_kernel, [(192, LANES)] + [message] * 4, [], [t, base, flags], 1000000
    )
    got = exchange(faces)
    s, *faces = call(
        first_kernel, [(640, LANES)] + [short] * 4, scratch, [t, coefs, wm, *got], 10000000
    )
    again = exchange(faces)
    (out,) = call(
        second_kernel, [(640, LANES)], scratch, [t, s, coefs, wm, *got, *again], 10000000
    )
    return out.reshape(tangent.shape)


def solution(mesh):
    in_specs = (P(None, None, "gx", "gy", None), P(None, "gx", "gy", None), P("gx", "gy", None))
    out_specs = P(None, None, "gx", "gy", None)
    return jax.shard_map(
        per_device, mesh=mesh, in_specs=in_specs, out_specs=out_specs, check_vma=False
    )
```

```python
import math

import jax
import jax.numpy as jnp
import numpy as np
from jax import lax
from jax.experimental import pallas as pl
from jax.experimental.pallas import tpu as pltpu
from jax.sharding import PartitionSpec as P

STEP = 0.1
COLS = 8
LANES = 128
V1, V2, V3, W1, W2, W3, KE, HH, SX, SY, SZ, NU = range(12)
FACE = 160
FACE_NAMES = (V1, V2, V3, KE, HH, NU)
COEF_ROWS = 32
ORDER_1 = (0, 1, 3, 2)
ORDER_2 = (1, 3, 0, 2)


def node_tables():
    inner_point = math.sqrt(0.2)
    points = [-1.0, -inner_point, inner_point, 1.0]
    weights = [1.0 / 6.0, 5.0 / 6.0, 5.0 / 6.0, 1.0 / 6.0]
    barycentric = []
    for j in range(4):
        product = 1.0
        for k in range(4):
            if k != j:
                product = product * (points[j] - points[k])
        barycentric.append(1.0 / product)
    deriv = [[0.0] * 4 for i in range(4)]
    for i in range(4):
        for j in range(4):
            if j != i:
                deriv[i][j] = barycentric[j] / barycentric[i] / (points[i] - points[j])
        deriv[i][i] = -sum((deriv[i][j] for j in range(4) if j != i))
    norms = [2.0, 2.0 / 3.0, 2.0 / 5.0, 2.0 / 3.0]
    legendre = [
        lambda x: 1.0,
        lambda x: x,
        lambda x: 0.5 * (3.0 * x * x - 1.0),
        lambda x: 0.5 * (5.0 * x * x * x - 3.0 * x),
    ]
    modal = [[weights[i] * legendre[k](points[i]) / norms[k] for i in range(4)] for k in range(4)]
    return deriv, modal


DERIV, MODAL = node_tables()


def span_table(wm_ref):
    k = lax.broadcasted_iota(jnp.int32, (LANES, LANES), 0)
    n = lax.broadcasted_iota(jnp.int32, (LANES, LANES), 1)
    place = (n % 4) * LANES + ((k - n) & (LANES - 1))
    hi = jnp.zeros((LANES, LANES), jnp.float32)
    lo = hi
    entries = [(i, j - i, DERIV[i][j]) for i in range(4) for j in range(4) if i != j]
    for i, offset, value in entries + [(0, -1, -3.0), (3, 1, 3.0)]:
        head = float(np.float32(value).astype(jnp.bfloat16))
        here = place == i * LANES + (offset & (LANES - 1))
        hi = jnp.where(here, head, hi)
        lo = jnp.where(here, value - head, lo)
    hi, lo = hi.astype(jnp.bfloat16), lo.astype(jnp.bfloat16)
    wm_ref[:LANES, :LANES] = hi
    wm_ref[LANES:, :LANES] = hi
    wm_ref[:LANES, LANES:] = lo
    wm_ref[LANES:, LANES:] = jnp.zeros_like(lo)


def row(f, x, y):
    return (f * 16 + x * 4 + y) * COLS


def face_row(f, n):
    return (f * 4 + n) * COLS


def tan_in(ref, f, x, y):
    return ref[pl.ds(f * 16 + x * 4 + y, COLS, stride=80), :]


def coef(ref, name, x, y):
    r = name * 16 + x * 4 + y
    return ref[r : r + 1, :]


def group_transform(f, matrix, axis, index, step):
    size = f.shape[axis]
    total = None
    for offset in range(-3, 4):
        c = jnp.zeros_like(f)
        for i in range(4):
            if 0 <= i + offset < 4:
                c = jnp.where(index == i, matrix[i][i + offset], c)
        moved = f if offset == 0 else pltpu.roll(f, (-offset * step) % size, axis)
        term = c * moved
        total = term if total is None else total + term
    return total


def base_coefs(base_ref, flags_ref, coef_ref):
    u = [base_ref[f * 16 : (f + 1) * 16, :] for f in range(5)]
    inv = 1.0 / u[0]
    v = [u[1 + d] * inv for d in range(3)]
    ke = 0.5 * (v[0] * v[0] + v[1] * v[1] + v[2] * v[2])
    pressure = 0.4 * (u[4] - ke * u[0])
    sound = jnp.sqrt(1.4 * pressure * inv)
    speed = [jnp.abs(v[d]) + sound for d in range(3)]
    lane = lax.broadcasted_iota(jnp.int32, (16, LANES), 1)
    sub = lax.broadcasted_iota(jnp.int32, (16, LANES), 0)
    zi, yi, xi = lane % 4, sub % 4, sub // 4
    near = jnp.where(
        zi == 3, pltpu.roll(speed[2], LANES - 1, 1), pltpu.roll(speed[2], 1, 1)
    )
    sz = jnp.where((zi == 0) | (zi == 3), 3.0 * jnp.maximum(speed[2], near), 0.0)
    modal = group_transform(u[0], MODAL, 1, zi, 1)
    modal = group_transform(modal, MODAL, 0, yi, 1)
    modal = group_transform(modal, MODAL, 0, xi, 4)
    squares = modal * modal
    edge = jnp.where((zi == 3) | (yi == 3) | (xi == 3), squares, 0.0)
    ones = [[1.0] * 4] * 4
    sums = []
    for s in (squares, edge):
        s = jnp.broadcast_to(jnp.sum(s, axis=0, keepdims=True), (8, LANES))
        sums.append(group_transform(s, ones, 1, zi[:8], 1))
    sensor = jnp.log(sums[1] / sums[0] + 1e-10) * (1.0 / math.log(10.0))
    shape = 1.0 / (1.0 + jnp.exp(-(sensor + 2.3) * 2.0))
    spread = jnp.where(
        lax.broadcasted_iota(jnp.int32, (32, LANES), 1) // 4
        == lax.broadcasted_iota(jnp.int32, (32, LANES), 0),
        1.0,
        0.0,
    )
    flags = jnp.broadcast_to(flags_ref[...].astype(jnp.float32), (8, 32))
    flags = jnp.dot(flags, spread, preferred_element_type=jnp.float32)
    nu = 0.1 * flags * shape
    nu = jnp.concatenate([nu, nu], axis=0)
    table = {
        V1: v[0], V2: v[1], V3: v[2],
        W1: 0.4 * v[0], W2: 0.4 * v[1], W3: 0.4 * v[2],
        KE: 0.4 * ke, HH: (u[4] + pressure) * inv,
        SX: speed[0], SY: speed[1], SZ: sz, NU: nu,
    }
    for name, value in table.items():
        coef_ref[name * 16 : (name + 1) * 16, :] = value


def pack_faces(load, outs, odd_x, odd_y):
    for axis, (near, far), odd in ((0, outs[:2], odd_x), (1, outs[2:], odd_y)):
        for f in range(5):
            for n in range(4):
                line = [load(f, k, n) if axis == 0 else load(f, n, k) for k in range(4)]
                lower = line[0] * DERIV[0][0]
                upper = line[3] * DERIV[3][3]
                for k in range(1, 4):
                    lower = lower + DERIV[0][k] * line[k]
                    upper = upper + DERIV[3][3 - k] * line[3 - k]
                r = face_row(f, n)
                near[r : r + 8, :] = jnp.where(odd, line[0], line[3])
                far[r : r + 8, :] = jnp.where(odd, line[3], line[0])
                near[FACE + r : FACE + r + 8, :] = jnp.where(odd, lower, upper)
                far[FACE + r : FACE + r + 8, :] = jnp.where(odd, upper, lower)


def by_face(refs, order):
    return tuple(refs[order.index(face)] for face in range(4))


def pack_kernel(t_hbm, base_hbm, flags_hbm, coef_ref, *refs):
    xn, xf, yn, yf = by_face(refs[:4], ORDER_1)
    t_ref, base_ref, flags_ref, sems = refs[4:]
    copies = [
        pltpu.make_async_copy(src, dst, sems.at[k])
        for k, (src, dst) in enumerate(
            ((base_hbm, base_ref), (flags_hbm, flags_ref), (t_hbm, t_ref))
        )
    ]
    for copy in copies:
        copy.start()
    odd_x = lax.axis_index("gx") % 2 == 1
    odd_y = lax.axis_index("gy") % 2 == 1
    copies[0].wait()
    copies[1].wait()
    base_coefs(base_ref, flags_ref, coef_ref)
    copies[2].wait()
    pack_faces(lambda f, x, y: tan_in(t_ref, f, x, y), (xn, xf, yn, yf), odd_x, odd_y)
    for axis, (near, far), odd in ((0, (xn, xf), odd_x), (1, (yn, yf), odd_y)):
        for place, name in enumerate(FACE_NAMES + (SX + axis,)):
            first = name * 16
            if axis == 0:
                lower = coef_ref[first : first + 4, :]
                upper = coef_ref[first + 12 : first + 16, :]
            else:
                lower = coef_ref[pl.ds(first, 4, stride=4), :]
                upper = coef_ref[pl.ds(first + 3, 4, stride=4), :]
            r = 2 * FACE + 4 * place
            near[r : r + 4, :] = jnp.where(odd, lower, upper)
            far[r : r + 4, :] = jnp.where(odd, upper, lower)
        r = 2 * FACE + 28
        near[r : r + 4, :] = jnp.zeros((4, LANES), jnp.float32)
        far[r : r + 4, :] = jnp.zeros((4, LANES), jnp.float32)


def flux(d, t, v, dp, e, hh):
    u = t[1 + d] - v[d] * t[0]
    out = [t[1 + d]]
    for i in range(3):
        value = v[d] * t[1 + i] + v[i] * u
        out.append(value + dp if i == d else value)
    out.append(v[d] * e + hh * u)
    return out


def volume(load, coef_ref, wm_ref, acc, ops, aux):
    top_lane = lax.broadcasted_iota(jnp.int32, (COLS, LANES), 1) % 4 == 3
    chunk = 128

    def put(f, x, y, value):
        hi = value.astype(jnp.bfloat16)
        r = row(f, x, y)
        ops[r : r + 16, :LANES] = hi
        ops[r : r + 16, LANES:] = (value - hi.astype(jnp.float32)).astype(jnp.bfloat16)

    def span_product():
        for c in range(640 // chunk):
            both = jnp.dot(
                ops[c * chunk : (c + 1) * chunk, :],
                wm_ref[...],
                preferred_element_type=jnp.float32,
            )
            acc[c * chunk : (c + 1) * chunk, :] = both[:, :LANES] + both[:, LANES:]

    for x in range(4):
        for f in range(5):
            for y in (0, 2):
                put(f, x, y, jnp.concatenate([load(f, x, y), load(f, x, y + 1)], axis=0))
    span_product()

    for x in range(4):
        for y in (0, 2):
            parts = []
            for yy in (y, y + 1):
                t = [load(f, x, yy) for f in range(5)]
                v = [coef(coef_ref, V1 + d, x, yy) for d in range(3)]
                w = [coef(coef_ref, W1 + d, x, yy) for d in range(3)]
                dp = 0.4 * t[4] + coef(coef_ref, KE, x, yy) * t[0]
                for d in range(3):
                    dp = dp - w[d] * t[1 + d]
                e = t[4] + dp
                k = (x * 4 + yy) * 16
                aux[k : k + 8, :] = dp
                aux[k + 8 : k + 16, :] = e
                g = flux(2, t, v, dp, e, coef(coef_ref, HH, x, yy))
                nu = coef(coef_ref, NU, x, yy)
                out = []
                for f in range(5):
                    r = row(f, x, yy)
                    out.append(nu * acc[r : r + 8, :] - g[f])
                parts.append(out)
            for f in range(5):
                put(f, x, y, jnp.concatenate([parts[0][f], parts[1][f]], axis=0))
    span_product()

    for axis in range(2):
        for n in range(4):
            line = [(k, n) if axis == 0 else (n, k) for k in range(4)]
            t = [[load(f, x, y) for f in range(5)] for x, y in line]
            g = []
            for k, (x, y) in enumerate(line):
                v = [coef(coef_ref, V1 + d, x, y) for d in range(3)]
                r = (x * 4 + y) * 16
                g.append(
                    flux(axis, t[k], v, aux[r : r + 8, :], aux[r + 8 : r + 16, :],
                         coef(coef_ref, HH, x, y))
                )
            nu = coef(coef_ref, NU, *line[0])
            for f in range(5):
                tt = [t[k][f] for k in range(4)]
                fl = []
                for i in range(4):
                    fl.append(nu * row_product(i, tt) - g[i][f])
                for i, (x, y) in enumerate(line):
                    r = row(f, x, y)
                    total = acc[r : r + 8, :] + row_product(i, fl)
                    if axis == 0:
                        other = jnp.where(
                            top_lane, pltpu.roll(tt[i], LANES - 1, 1), pltpu.roll(tt[i], 1, 1)
                        )
                        total = total + coef(coef_ref, SZ, x, y) * (other - tt[i])
                    acc[r : r + 8, :] = total


def row_product(i, values):
    total = None
    for k in range(4):
        if k != i:
            term = DERIV[i][k] * values[k]
            total = term if total is None else total + term
    return total


def add_faces(load, coef_ref, recv, coef_recv, odd_x, odd_y, acc, work, finish):
    for axis, odd in ((0, odd_x), (1, odd_y)):
        near, far = recv[2 * axis : 2 * axis + 2]
        near_c, far_c = coef_recv[2 * axis : 2 * axis + 2]

        def pick(low, r, rows=8):
            a, b = near[r : r + rows, :], far[r : r + rows, :]
            return jnp.where(odd, a, b) if low else jnp.where(odd, b, a)

        def pick_coef(low, place, n):
            r = 2 * FACE + 4 * place + n
            a, b = near_c[r : r + 1, :], far_c[r : r + 1, :]
            return jnp.where(odd, a, b) if low else jnp.where(odd, b, a)

        for n in range(4):
            line = [(k, n) if axis == 0 else (n, k) for k in range(4)]
            nu3 = 3.0 * coef(coef_ref, NU, *line[0])
            shift, extra = [], []
            for low in (True, False):
                place = line[0] if low else line[3]
                far_t = [pick(low, face_row(f, n)) for f in range(5)]
                v = [pick_coef(low, d, n) for d in range(3)]
                dp = 0.4 * far_t[4] + pick_coef(low, 3, n) * far_t[0]
                for d in range(3):
                    dp = dp - (0.4 * v[d]) * far_t[1 + d]
                far_g = flux(axis, far_t, v, dp, far_t[4] + dp, pick_coef(low, 4, n))
                far_nu = pick_coef(low, 5, n)
                s3 = 3.0 * jnp.maximum(
                    coef(coef_ref, SX + axis, *place), pick_coef(low, 6, n)
                )
                moved, added = [], []
                for f in range(5):
                    gap = far_t[f] - load(f, *place)
                    far_d = pick(low, FACE + face_row(f, n))
                    far_q = far_d - 3.0 * gap if low else far_d + 3.0 * gap
                    value = 3.0 * (far_nu * far_q - far_g[f])
                    added.append(s3 * gap - value if low else s3 * gap + value)
                    moved.append(-(nu3 * far_t[f]) if low else nu3 * far_t[f])
                shift.append(moved)
                extra.append(added)
            for f in range(5):
                for i, (x, y) in enumerate(line):
                    r = row(f, x, y)
                    total = (acc if axis == 0 else work)[r : r + 8, :]
                    if i != 0:
                        total = total + DERIV[i][0] * shift[0][f]
                    if i != 3:
                        total = total + DERIV[i][3] * shift[1][f]
                    if i == 0:
                        total = total + extra[0][f]
                    if i == 3:
                        total = total + extra[1][f]
                    if axis == 0:
                        work[r : r + 8, :] = total
                    else:
                        finish(f, x, y, total)


def loader(ref):
    def load(f, x, y):
        r = row(f, x, y)
        return ref[r : r + 8, :]

    return load


def first_volume(t_ref, coef_ref, acc, wm_ref, ops, aux):
    span_table(wm_ref)
    volume(lambda f, x, y: tan_in(t_ref, f, x, y), coef_ref, wm_ref, acc, ops, aux)


def second_volume(s_ref, coef_ref, wm_ref, acc, ops, aux):
    volume(loader(s_ref), coef_ref, wm_ref, acc, ops, aux)


def first_faces(t_ref, coef_ref, acc, r0, r1, r2, r3, s_ref, m0, m1, m2, m3, work):
    odd_x = lax.axis_index("gx") % 2 == 1
    odd_y = lax.axis_index("gy") % 2 == 1
    load = lambda f, x, y: tan_in(t_ref, f, x, y)

    def finish(f, x, y, total):
        r = row(f, x, y)
        s_ref[r : r + 8, :] = load(f, x, y) + STEP * total

    faces = by_face((r0, r1, r2, r3), ORDER_1)
    add_faces(load, coef_ref, faces, faces, odd_x, odd_y, acc, work, finish)
    pack_faces(loader(s_ref), by_face((m0, m1, m2, m3), ORDER_2), odd_x, odd_y)


def second_faces(
    t_ref, s_ref, coef_ref, acc, c0, c1, c2, c3, r0, r1, r2, r3, out_ref, work
):
    odd_x = lax.axis_index("gx") % 2 == 1
    odd_y = lax.axis_index("gy") % 2 == 1
    load = loader(s_ref)

    def finish(f, x, y, total):
        value = 0.5 * tan_in(t_ref, f, x, y) + (0.5 * load(f, x, y) + (0.5 * STEP) * total)
        out_ref[pl.ds(f * 16 + x * 4 + y, COLS, stride=80), :] = value

    add_faces(
        load, coef_ref, by_face((r0, r1, r2, r3), ORDER_2),
        by_face((c0, c1, c2, c3), ORDER_1), odd_x, odd_y, acc, work, finish,
    )


def call(kernel, shapes, scratch, args, flops, space=pltpu.VMEM, limit=16):
    return pl.pallas_call(
        kernel,
        out_shape=[
            s if hasattr(s, "dtype") else jax.ShapeDtypeStruct(s, jnp.float32) for s in shapes
        ],
        in_specs=[pl.BlockSpec(memory_space=space)] * len(args),
        out_specs=[pl.BlockSpec(memory_space=pltpu.VMEM)] * len(shapes),
        scratch_shapes=scratch,
        compiler_params=pltpu.CompilerParams(vmem_limit_bytes=limit * 1024 * 1024),
        cost_estimate=pl.CostEstimate(flops=flops, bytes_accessed=1000000, transcendentals=0),
    )(*args)


def exchange(messages, order):
    size_x, size_y = lax.axis_size("gx"), lax.axis_size("gy")

    def pairs(size, first):
        out = []
        for i in range(first, size - 1, 2):
            out += [(i, i + 1), (i + 1, i)]
        if first == 1:
            out += [(0, 0)]
            if size % 2 == 0:
                out += [(size - 1, size - 1)]
        return out

    plan = (
        ("gx", pairs(size_x, 0)),
        ("gx", pairs(size_x, 1)),
        ("gy", pairs(size_y, 0)),
        ("gy", pairs(size_y, 1)),
    )
    return [lax.ppermute(m, *plan[face]) for m, face in zip(messages, order)]


def per_device(tangent, base_state, shock_flags):
    t = tangent.reshape(640, LANES)
    base = base_state.reshape(80, LANES)
    flags = shock_flags.reshape(1, 32)
    message = (2 * FACE + COEF_ROWS, LANES)
    short = (2 * FACE, LANES)
    whole = (640, LANES)
    volume_scratch = [
        pltpu.VMEM((640, 2 * LANES), jnp.bfloat16),
        pltpu.VMEM((256, LANES), jnp.float32),
    ]
    work = [pltpu.VMEM(whole, jnp.float32)]
    staging = [
        pltpu.VMEM(whole, jnp.float32),
        pltpu.VMEM(base.shape, jnp.float32),
        pltpu.VMEM(flags.shape, jnp.int32),
        pltpu.SemaphoreType.DMA((3,)),
    ]
    coefs, *faces = call(
        pack_kernel, [(192, LANES)] + [message] * 4, staging, [t, base, flags], 1000000,
        space=pltpu.HBM, limit=56,
    )
    got = exchange(faces, ORDER_1)
    inner, wm = call(
        first_volume, [whole, jax.ShapeDtypeStruct((256, 256), jnp.bfloat16)], volume_scratch, [t, coefs],
        10000000,
    )
    s, *faces = call(
        first_faces, [whole] + [short] * 4, work, [t, coefs, inner, *got], 1000000
    )
    again = exchange(faces, ORDER_2)
    (inner,) = call(second_volume, [whole], volume_scratch, [s, coefs, wm], 10000000)
    (out,) = call(second_faces, [whole], work, [t, s, coefs, inner, *got, *again], 1000000)
    return out.reshape(tangent.shape)


def solution(mesh):
    in_specs = (P(None, None, "gx", "gy", None), P(None, "gx", "gy", None), P("gx", "gy", None))
    out_specs = P(None, None, "gx", "gy", None)
    return jax.shard_map(
        per_device, mesh=mesh, in_specs=in_specs, out_specs=out_specs, check_vma=False
    )
```

```python
import math

import jax
import jax.numpy as jnp
import numpy as np
from jax import lax
from jax.experimental import pallas as pl
from jax.experimental.pallas import tpu as pltpu
from jax.sharding import PartitionSpec as P

STEP = 0.1
COLS = 8
LANES = 128
V1, V2, V3, W1, W2, W3, KE, HH, SX, SY, SZ, NU = range(12)
FACE = 160
HALF = 80
FACE_NAMES = (V1, V2, V3, KE, HH, NU)
COEF_ROWS = 32
COEF_AT = FACE + HALF
PLACE_AT = 12 * 16
ORDER_1 = (0, 1, 3, 2)
ORDER_2 = (1, 3, 0, 2)


def node_tables():
    inner_point = math.sqrt(0.2)
    points = [-1.0, -inner_point, inner_point, 1.0]
    weights = [1.0 / 6.0, 5.0 / 6.0, 5.0 / 6.0, 1.0 / 6.0]
    barycentric = []
    for j in range(4):
        product = 1.0
        for k in range(4):
            if k != j:
                product = product * (points[j] - points[k])
        barycentric.append(1.0 / product)
    deriv = [[0.0] * 4 for i in range(4)]
    for i in range(4):
        for j in range(4):
            if j != i:
                deriv[i][j] = barycentric[j] / barycentric[i] / (points[i] - points[j])
        deriv[i][i] = -sum((deriv[i][j] for j in range(4) if j != i))
    norms = [2.0, 2.0 / 3.0, 2.0 / 5.0, 2.0 / 3.0]
    legendre = [
        lambda x: 1.0,
        lambda x: x,
        lambda x: 0.5 * (3.0 * x * x - 1.0),
        lambda x: 0.5 * (5.0 * x * x * x - 3.0 * x),
    ]
    modal = [[weights[i] * legendre[k](points[i]) / norms[k] for i in range(4)] for k in range(4)]
    return deriv, modal


DERIV, MODAL = node_tables()


def span_table(wm_ref):
    k = lax.broadcasted_iota(jnp.int32, (LANES, LANES), 0)
    n = lax.broadcasted_iota(jnp.int32, (LANES, LANES), 1)
    place = (n % 4) * LANES + ((k - n) & (LANES - 1))
    hi = jnp.zeros((LANES, LANES), jnp.float32)
    lo = hi
    entries = [(i, j - i, DERIV[i][j]) for i in range(4) for j in range(4) if i != j]
    for i, offset, value in entries + [(0, -1, -3.0), (3, 1, 3.0)]:
        head = float(np.float32(value).astype(jnp.bfloat16))
        here = place == i * LANES + (offset & (LANES - 1))
        hi = jnp.where(here, head, hi)
        lo = jnp.where(here, value - head, lo)
    hi, lo = hi.astype(jnp.bfloat16), lo.astype(jnp.bfloat16)
    wm_ref[:LANES, :LANES] = hi
    wm_ref[LANES:, :LANES] = hi
    wm_ref[:LANES, LANES:] = lo
    wm_ref[LANES:, LANES:] = jnp.zeros_like(lo)


def row(f, x, y):
    return (f * 16 + x * 4 + y) * COLS


def face_row(f, n):
    return (f * 4 + n) * COLS


def tan_in(ref, f, x, y):
    return ref[pl.ds(f * 16 + x * 4 + y, COLS, stride=80), :]


def coef(ref, name, x, y):
    r = name * 16 + x * 4 + y
    return ref[r : r + 1, :]


def group_transform(f, matrix, axis, index, step):
    size = f.shape[axis]
    total = None
    for offset in range(-3, 4):
        c = jnp.zeros_like(f)
        for i in range(4):
            if 0 <= i + offset < 4:
                c = jnp.where(index == i, matrix[i][i + offset], c)
        moved = f if offset == 0 else pltpu.roll(f, (-offset * step) % size, axis)
        term = c * moved
        total = term if total is None else total + term
    return total


def base_coefs(base_ref, flags_ref, coef_ref):
    u = [base_ref[f * 16 : (f + 1) * 16, :] for f in range(5)]
    inv = 1.0 / u[0]
    v = [u[1 + d] * inv for d in range(3)]
    ke = 0.5 * (v[0] * v[0] + v[1] * v[1] + v[2] * v[2])
    pressure = 0.4 * (u[4] - ke * u[0])
    sound = jnp.sqrt(1.4 * pressure * inv)
    speed = [jnp.abs(v[d]) + sound for d in range(3)]
    lane = lax.broadcasted_iota(jnp.int32, (16, LANES), 1)
    sub = lax.broadcasted_iota(jnp.int32, (16, LANES), 0)
    zi, yi, xi = lane % 4, sub % 4, sub // 4
    near = jnp.where(
        zi == 3, pltpu.roll(speed[2], LANES - 1, 1), pltpu.roll(speed[2], 1, 1)
    )
    sz = jnp.where((zi == 0) | (zi == 3), 3.0 * jnp.maximum(speed[2], near), 0.0)
    modal = group_transform(u[0], MODAL, 1, zi, 1)
    modal = group_transform(modal, MODAL, 0, yi, 1)
    modal = group_transform(modal, MODAL, 0, xi, 4)
    squares = modal * modal
    edge = jnp.where((zi == 3) | (yi == 3) | (xi == 3), squares, 0.0)
    ones = [[1.0] * 4] * 4
    sums = []
    for s in (squares, edge):
        s = jnp.broadcast_to(jnp.sum(s, axis=0, keepdims=True), (8, LANES))
        sums.append(group_transform(s, ones, 1, zi[:8], 1))
    sensor = jnp.log(sums[1] / sums[0] + 1e-10) * (1.0 / math.log(10.0))
    shape = 1.0 / (1.0 + jnp.exp(-(sensor + 2.3) * 2.0))
    spread = jnp.where(
        lax.broadcasted_iota(jnp.int32, (32, LANES), 1) // 4
        == lax.broadcasted_iota(jnp.int32, (32, LANES), 0),
        1.0,
        0.0,
    )
    element_flags = jnp.broadcast_to(flags_ref[...].astype(jnp.float32), (8, 32))
    flags = jnp.dot(element_flags, spread, preferred_element_type=jnp.float32)
    ahead = jnp.where(
        lax.broadcasted_iota(jnp.int32, (32, LANES), 1) // 4
        > lax.broadcasted_iota(jnp.int32, (32, LANES), 0),
        1.0,
        0.0,
    )
    rank = jnp.dot(element_flags, ahead, preferred_element_type=jnp.float32)
    place = 4.0 * rank + zi[:8].astype(jnp.float32)
    coef_ref[PLACE_AT : PLACE_AT + 8, :] = jnp.where(flags > 0.5, place, -1000.0)
    nu = 0.1 * flags * shape
    nu = jnp.concatenate([nu, nu], axis=0)
    table = {
        V1: v[0], V2: v[1], V3: v[2],
        W1: 0.4 * v[0], W2: 0.4 * v[1], W3: 0.4 * v[2],
        KE: 0.4 * ke, HH: (u[4] + pressure) * inv,
        SX: speed[0], SY: speed[1], SZ: sz, NU: nu,
    }
    for name, value in table.items():
        coef_ref[name * 16 : (name + 1) * 16, :] = value


def selection(place):
    m = lax.broadcasted_iota(jnp.int32, (LANES, LANES), 0).astype(jnp.float32)
    lower = jnp.where(m == place, 1.0, 0.0).astype(jnp.bfloat16)
    upper = jnp.where(m == place + 64.0, 1.0, 0.0).astype(jnp.bfloat16)
    return jnp.concatenate([lower, upper], axis=1)


def select(value, chosen, dims):
    hi = value.astype(jnp.bfloat16)
    lo = (value - hi.astype(jnp.float32)).astype(jnp.bfloat16)
    return sum(
        lax.dot_general(part, chosen, (dims, ((), ())), preferred_element_type=jnp.float32)
        for part in (hi, lo)
    )


def wide_at(face, f, n):
    item = f * 4 + n
    r, c = face * HALF + (item % 10) * 8, (item // 10) * LANES
    return slice(r, r + 8), slice(c, c + LANES)


def pack_faces(load, coef_ref, outs, odd_x, odd_y, wide):
    for axis, (near, far), odd in ((0, outs[:2], odd_x), (1, outs[2:], odd_y)):
        for f in range(5):
            for n in range(4):
                line = [load(f, k, n) if axis == 0 else load(f, n, k) for k in range(4)]
                lower = line[0] * DERIV[0][0]
                upper = line[3] * DERIV[3][3]
                for k in range(1, 4):
                    lower = lower + DERIV[0][k] * line[k]
                    upper = upper + DERIV[3][3 - k] * line[3 - k]
                r = face_row(f, n)
                near[r : r + 8, :] = jnp.where(odd, line[0], line[3])
                far[r : r + 8, :] = jnp.where(odd, line[3], line[0])
                wide[wide_at(2 * axis, f, n)] = jnp.where(odd, lower, upper)
                wide[wide_at(2 * axis + 1, f, n)] = jnp.where(odd, upper, lower)
    chosen = selection(coef_ref[PLACE_AT : PLACE_AT + 1, :])
    for face in range(4):
        rows = wide[face * HALF : (face + 1) * HALF, :]
        outs[face][FACE:COEF_AT, :] = select(rows, chosen, ((1,), (1,)))


def by_face(refs, order):
    return tuple(refs[order.index(face)] for face in range(4))


def pack_kernel(t_hbm, base_hbm, flags_hbm, coef_ref, *refs):
    xn, xf, yn, yf = by_face(refs[:4], ORDER_1)
    t_ref, base_ref, flags_ref, wide, sems = refs[4:]
    copies = [
        pltpu.make_async_copy(src, dst, sems.at[k])
        for k, (src, dst) in enumerate(
            ((base_hbm, base_ref), (flags_hbm, flags_ref), (t_hbm, t_ref))
        )
    ]
    for copy in copies:
        copy.start()
    odd_x = lax.axis_index("gx") % 2 == 1
    odd_y = lax.axis_index("gy") % 2 == 1
    copies[0].wait()
    copies[1].wait()
    base_coefs(base_ref, flags_ref, coef_ref)
    copies[2].wait()
    faces = (xn, xf, yn, yf)
    load = lambda f, x, y: tan_in(t_ref, f, x, y)
    pack_faces(load, coef_ref, faces, odd_x, odd_y, wide)
    for axis, (near, far), odd in ((0, (xn, xf), odd_x), (1, (yn, yf), odd_y)):
        for place, name in enumerate(FACE_NAMES + (SX + axis,)):
            first = name * 16
            if axis == 0:
                lower = coef_ref[first : first + 4, :]
                upper = coef_ref[first + 12 : first + 16, :]
            else:
                lower = coef_ref[pl.ds(first, 4, stride=4), :]
                upper = coef_ref[pl.ds(first + 3, 4, stride=4), :]
            r = COEF_AT + 4 * place
            near[r : r + 4, :] = jnp.where(odd, lower, upper)
            far[r : r + 4, :] = jnp.where(odd, upper, lower)
        r = COEF_AT + 28
        near[r : r + 4, :] = coef_ref[PLACE_AT : PLACE_AT + 4, :]
        far[r : r + 4, :] = coef_ref[PLACE_AT : PLACE_AT + 4, :]


def flux(d, t, v, dp, e, hh):
    u = t[1 + d] - v[d] * t[0]
    out = [t[1 + d]]
    for i in range(3):
        value = v[d] * t[1 + i] + v[i] * u
        out.append(value + dp if i == d else value)
    out.append(v[d] * e + hh * u)
    return out


def volume(load, coef_ref, wm_ref, acc, ops, aux):
    top_lane = lax.broadcasted_iota(jnp.int32, (COLS, LANES), 1) % 4 == 3
    chunk = 128

    def put(f, x, y, value):
        hi = value.astype(jnp.bfloat16)
        r = row(f, x, y)
        ops[r : r + 16, :LANES] = hi
        ops[r : r + 16, LANES:] = (value - hi.astype(jnp.float32)).astype(jnp.bfloat16)

    def span_product():
        for c in range(640 // chunk):
            both = jnp.dot(
                ops[c * chunk : (c + 1) * chunk, :],
                wm_ref[...],
                preferred_element_type=jnp.float32,
            )
            acc[c * chunk : (c + 1) * chunk, :] = both[:, :LANES] + both[:, LANES:]

    for x in range(4):
        for f in range(5):
            for y in (0, 2):
                put(f, x, y, jnp.concatenate([load(f, x, y), load(f, x, y + 1)], axis=0))
    span_product()

    for x in range(4):
        for y in (0, 2):
            parts = []
            for yy in (y, y + 1):
                t = [load(f, x, yy) for f in range(5)]
                v = [coef(coef_ref, V1 + d, x, yy) for d in range(3)]
                w = [coef(coef_ref, W1 + d, x, yy) for d in range(3)]
                dp = 0.4 * t[4] + coef(coef_ref, KE, x, yy) * t[0]
                for d in range(3):
                    dp = dp - w[d] * t[1 + d]
                e = t[4] + dp
                k = (x * 4 + yy) * 16
                aux[k : k + 8, :] = dp
                aux[k + 8 : k + 16, :] = e
                g = flux(2, t, v, dp, e, coef(coef_ref, HH, x, yy))
                nu = coef(coef_ref, NU, x, yy)
                out = []
                for f in range(5):
                    r = row(f, x, yy)
                    out.append(nu * acc[r : r + 8, :] - g[f])
                parts.append(out)
            for f in range(5):
                put(f, x, y, jnp.concatenate([parts[0][f], parts[1][f]], axis=0))
    span_product()

    for axis in range(2):
        for n in range(4):
            line = [(k, n) if axis == 0 else (n, k) for k in range(4)]
            t = [[load(f, x, y) for f in range(5)] for x, y in line]
            g = []
            for k, (x, y) in enumerate(line):
                v = [coef(coef_ref, V1 + d, x, y) for d in range(3)]
                r = (x * 4 + y) * 16
                g.append(
                    flux(axis, t[k], v, aux[r : r + 8, :], aux[r + 8 : r + 16, :],
                         coef(coef_ref, HH, x, y))
                )
            nu = coef(coef_ref, NU, *line[0])
            for f in range(5):
                tt = [t[k][f] for k in range(4)]
                fl = []
                for i in range(4):
                    fl.append(nu * row_product(i, tt) - g[i][f])
                for i, (x, y) in enumerate(line):
                    r = row(f, x, y)
                    total = acc[r : r + 8, :] + row_product(i, fl)
                    if axis == 0:
                        other = jnp.where(
                            top_lane, pltpu.roll(tt[i], LANES - 1, 1), pltpu.roll(tt[i], 1, 1)
                        )
                        total = total + coef(coef_ref, SZ, x, y) * (other - tt[i])
                    acc[r : r + 8, :] = total


def row_product(i, values):
    total = None
    for k in range(4):
        if k != i:
            term = DERIV[i][k] * values[k]
            total = term if total is None else total + term
    return total


def add_faces(load, coef_ref, recv, coef_recv, odd_x, odd_y, acc, work, wide, finish):
    for face in range(4):
        r = COEF_AT + 28
        chosen = selection(coef_recv[face][r : r + 1, :])
        wide[face * HALF : (face + 1) * HALF, :] = select(
            recv[face][FACE:COEF_AT, :], chosen, ((1,), (0,))
        )
    for axis, odd in ((0, odd_x), (1, odd_y)):
        near, far = recv[2 * axis : 2 * axis + 2]
        near_c, far_c = coef_recv[2 * axis : 2 * axis + 2]

        def pick(low, r, rows=8):
            a, b = near[r : r + rows, :], far[r : r + rows, :]
            return jnp.where(odd, a, b) if low else jnp.where(odd, b, a)

        def pick_coef(low, place, n):
            r = COEF_AT + 4 * place + n
            a, b = near_c[r : r + 1, :], far_c[r : r + 1, :]
            return jnp.where(odd, a, b) if low else jnp.where(odd, b, a)

        for n in range(4):
            line = [(k, n) if axis == 0 else (n, k) for k in range(4)]
            nu3 = 3.0 * coef(coef_ref, NU, *line[0])
            shift, extra = [], []
            for low in (True, False):
                place = line[0] if low else line[3]
                far_t = [pick(low, face_row(f, n)) for f in range(5)]
                v = [pick_coef(low, d, n) for d in range(3)]
                dp = 0.4 * far_t[4] + pick_coef(low, 3, n) * far_t[0]
                for d in range(3):
                    dp = dp - (0.4 * v[d]) * far_t[1 + d]
                far_g = flux(axis, far_t, v, dp, far_t[4] + dp, pick_coef(low, 4, n))
                far_nu = pick_coef(low, 5, n)
                s3 = 3.0 * jnp.maximum(
                    coef(coef_ref, SX + axis, *place), pick_coef(low, 6, n)
                )
                moved, added = [], []
                for f in range(5):
                    gap = far_t[f] - load(f, *place)
                    a = wide[wide_at(2 * axis, f, n)]
                    b = wide[wide_at(2 * axis + 1, f, n)]
                    far_d = jnp.where(odd, a, b) if low else jnp.where(odd, b, a)
                    far_q = far_d - 3.0 * gap if low else far_d + 3.0 * gap
                    value = 3.0 * (far_nu * far_q - far_g[f])
                    added.append(s3 * gap - value if low else s3 * gap + value)
                    moved.append(-(nu3 * far_t[f]) if low else nu3 * far_t[f])
                shift.append(moved)
                extra.append(added)
            for f in range(5):
                for i, (x, y) in enumerate(line):
                    r = row(f, x, y)
                    total = (acc if axis == 0 else work)[r : r + 8, :]
                    if i != 0:
                        total = total + DERIV[i][0] * shift[0][f]
                    if i != 3:
                        total = total + DERIV[i][3] * shift[1][f]
                    if i == 0:
                        total = total + extra[0][f]
                    if i == 3:
                        total = total + extra[1][f]
                    if axis == 0:
                        work[r : r + 8, :] = total
                    else:
                        finish(f, x, y, total)


def loader(ref):
    def load(f, x, y):
        r = row(f, x, y)
        return ref[r : r + 8, :]

    return load


def first_volume(t_ref, coef_ref, acc, wm_ref, ops, aux):
    span_table(wm_ref)
    volume(lambda f, x, y: tan_in(t_ref, f, x, y), coef_ref, wm_ref, acc, ops, aux)


def second_volume(s_ref, coef_ref, wm_ref, acc, ops, aux):
    volume(loader(s_ref), coef_ref, wm_ref, acc, ops, aux)


def first_faces(t_ref, coef_ref, acc, r0, r1, r2, r3, s_ref, m0, m1, m2, m3, work, wide):
    odd_x = lax.axis_index("gx") % 2 == 1
    odd_y = lax.axis_index("gy") % 2 == 1
    load = lambda f, x, y: tan_in(t_ref, f, x, y)

    def finish(f, x, y, total):
        r = row(f, x, y)
        s_ref[r : r + 8, :] = load(f, x, y) + STEP * total

    faces = by_face((r0, r1, r2, r3), ORDER_1)
    add_faces(load, coef_ref, faces, faces, odd_x, odd_y, acc, work, wide, finish)
    sent = by_face((m0, m1, m2, m3), ORDER_2)
    pack_faces(loader(s_ref), coef_ref, sent, odd_x, odd_y, wide)


def second_faces(
    t_ref, s_ref, coef_ref, acc, c0, c1, c2, c3, r0, r1, r2, r3, out_ref, work, wide
):
    odd_x = lax.axis_index("gx") % 2 == 1
    odd_y = lax.axis_index("gy") % 2 == 1
    load = loader(s_ref)

    def finish(f, x, y, total):
        value = 0.5 * tan_in(t_ref, f, x, y) + (0.5 * load(f, x, y) + (0.5 * STEP) * total)
        out_ref[pl.ds(f * 16 + x * 4 + y, COLS, stride=80), :] = value

    add_faces(
        load, coef_ref, by_face((r0, r1, r2, r3), ORDER_2),
        by_face((c0, c1, c2, c3), ORDER_1), odd_x, odd_y, acc, work, wide, finish,
    )


def call(kernel, shapes, scratch, args, flops, space=pltpu.VMEM, limit=16):
    return pl.pallas_call(
        kernel,
        out_shape=[
            s if hasattr(s, "dtype") else jax.ShapeDtypeStruct(s, jnp.float32) for s in shapes
        ],
        in_specs=[pl.BlockSpec(memory_space=space)] * len(args),
        out_specs=[pl.BlockSpec(memory_space=pltpu.VMEM)] * len(shapes),
        scratch_shapes=scratch,
        compiler_params=pltpu.CompilerParams(vmem_limit_bytes=limit * 1024 * 1024),
        cost_estimate=pl.CostEstimate(flops=flops, bytes_accessed=1000000, transcendentals=0),
    )(*args)


def exchange(messages, order):
    size_x, size_y = lax.axis_size("gx"), lax.axis_size("gy")

    def pairs(size, first):
        out = []
        for i in range(first, size - 1, 2):
            out += [(i, i + 1), (i + 1, i)]
        if first == 1:
            out += [(0, 0)]
            if size % 2 == 0:
                out += [(size - 1, size - 1)]
        return out

    plan = (
        ("gx", pairs(size_x, 0)),
        ("gx", pairs(size_x, 1)),
        ("gy", pairs(size_y, 0)),
        ("gy", pairs(size_y, 1)),
    )
    return [lax.ppermute(m, *plan[face]) for m, face in zip(messages, order)]


def per_device(tangent, base_state, shock_flags):
    t = tangent.reshape(640, LANES)
    base = base_state.reshape(80, LANES)
    flags = shock_flags.reshape(1, 32)
    message = (COEF_AT + COEF_ROWS, LANES)
    short = (COEF_AT, LANES)
    whole = (640, LANES)
    volume_scratch = [
        pltpu.VMEM((640, 2 * LANES), jnp.bfloat16),
        pltpu.VMEM((256, LANES), jnp.float32),
    ]
    wide = pltpu.VMEM((4 * HALF, 2 * LANES), jnp.float32)
    work = [pltpu.VMEM(whole, jnp.float32), wide]
    staging = [
        pltpu.VMEM(whole, jnp.float32),
        pltpu.VMEM(base.shape, jnp.float32),
        pltpu.VMEM(flags.shape, jnp.int32),
        wide,
        pltpu.SemaphoreType.DMA((3,)),
    ]
    coefs, *faces = call(
        pack_kernel, [(PLACE_AT + 8, LANES)] + [message] * 4, staging, [t, base, flags], 1000000,
        space=pltpu.HBM, limit=56,
    )
    got = exchange(faces, ORDER_1)
    inner, wm = call(
        first_volume, [whole, jax.ShapeDtypeStruct((256, 256), jnp.bfloat16)], volume_scratch, [t, coefs],
        10000000,
    )
    s, *faces = call(
        first_faces, [whole] + [short] * 4, work, [t, coefs, inner, *got], 1000000
    )
    again = exchange(faces, ORDER_2)
    (inner,) = call(second_volume, [whole], volume_scratch, [s, coefs, wm], 10000000)
    (out,) = call(second_faces, [whole], work, [t, s, coefs, inner, *got, *again], 1000000)
    return out.reshape(tangent.shape)


def solution(mesh):
    in_specs = (P(None, None, "gx", "gy", None), P(None, "gx", "gy", None), P("gx", "gy", None))
    out_specs = P(None, None, "gx", "gy", None)
    return jax.shard_map(
        per_device, mesh=mesh, in_specs=in_specs, out_specs=out_specs, check_vma=False
    )
```

```python
import math

import jax
import jax.numpy as jnp
import numpy as np
from jax import lax
from jax.experimental import pallas as pl
from jax.experimental.pallas import tpu as pltpu
from jax.sharding import PartitionSpec as P

STEP = 0.1
COLS = 8
LANES = 128
V1, V2, V3, W1, W2, W3, KE, HH, SX, SY, SZ, NU = range(12)
FACE = 160
HALF = 80
FACE_NAMES = (V1, V2, V3, KE, HH, NU)
COEF_ROWS = 32
COEF_AT = FACE + HALF
PLACE_AT = 12 * 16
ORDER_1 = (1, 3, 0, 2)
ORDER_2 = (1, 3, 0, 2)


def node_tables():
    inner_point = math.sqrt(0.2)
    points = [-1.0, -inner_point, inner_point, 1.0]
    weights = [1.0 / 6.0, 5.0 / 6.0, 5.0 / 6.0, 1.0 / 6.0]
    barycentric = []
    for j in range(4):
        product = 1.0
        for k in range(4):
            if k != j:
                product = product * (points[j] - points[k])
        barycentric.append(1.0 / product)
    deriv = [[0.0] * 4 for i in range(4)]
    for i in range(4):
        for j in range(4):
            if j != i:
                deriv[i][j] = barycentric[j] / barycentric[i] / (points[i] - points[j])
        deriv[i][i] = -sum((deriv[i][j] for j in range(4) if j != i))
    norms = [2.0, 2.0 / 3.0, 2.0 / 5.0, 2.0 / 3.0]
    legendre = [
        lambda x: 1.0,
        lambda x: x,
        lambda x: 0.5 * (3.0 * x * x - 1.0),
        lambda x: 0.5 * (5.0 * x * x * x - 3.0 * x),
    ]
    modal = [[weights[i] * legendre[k](points[i]) / norms[k] for i in range(4)] for k in range(4)]
    return deriv, modal


DERIV, MODAL = node_tables()


def span_table(wm_ref):
    k = lax.broadcasted_iota(jnp.int32, (LANES, LANES), 0)
    n = lax.broadcasted_iota(jnp.int32, (LANES, LANES), 1)
    place = (n % 4) * LANES + ((k - n) & (LANES - 1))
    hi = jnp.zeros((LANES, LANES), jnp.float32)
    lo = hi
    entries = [(i, j - i, DERIV[i][j]) for i in range(4) for j in range(4) if i != j]
    for i, offset, value in entries + [(0, -1, -3.0), (3, 1, 3.0)]:
        head = float(np.float32(value).astype(jnp.bfloat16))
        here = place == i * LANES + (offset & (LANES - 1))
        hi = jnp.where(here, head, hi)
        lo = jnp.where(here, value - head, lo)
    hi, lo = hi.astype(jnp.bfloat16), lo.astype(jnp.bfloat16)
    wm_ref[:LANES, :LANES] = hi
    wm_ref[LANES:, :LANES] = hi
    wm_ref[:LANES, LANES:] = lo
    wm_ref[LANES:, LANES:] = jnp.zeros_like(lo)


def row(f, x, y):
    return (f * 16 + x * 4 + y) * COLS


def face_row(f, n):
    return (f * 4 + n) * COLS


def tan_in(ref, f, x, y):
    return ref[pl.ds(f * 16 + x * 4 + y, COLS, stride=80), :]


def coef(ref, name, x, y):
    r = name * 16 + x * 4 + y
    return ref[r : r + 1, :]


def group_transform(f, matrix, axis, index, step):
    size = f.shape[axis]
    total = None
    for offset in range(-3, 4):
        c = jnp.zeros_like(f)
        for i in range(4):
            if 0 <= i + offset < 4:
                c = jnp.where(index == i, matrix[i][i + offset], c)
        moved = f if offset == 0 else pltpu.roll(f, (-offset * step) % size, axis)
        term = c * moved
        total = term if total is None else total + term
    return total


def base_coefs(base_ref, flags_ref, coef_ref):
    u = [base_ref[f * 16 : (f + 1) * 16, :] for f in range(5)]
    inv = 1.0 / u[0]
    v = [u[1 + d] * inv for d in range(3)]
    ke = 0.5 * (v[0] * v[0] + v[1] * v[1] + v[2] * v[2])
    pressure = 0.4 * (u[4] - ke * u[0])
    sound = jnp.sqrt(1.4 * pressure * inv)
    speed = [jnp.abs(v[d]) + sound for d in range(3)]
    lane = lax.broadcasted_iota(jnp.int32, (16, LANES), 1)
    sub = lax.broadcasted_iota(jnp.int32, (16, LANES), 0)
    zi, yi, xi = lane % 4, sub % 4, sub // 4
    near = jnp.where(
        zi == 3, pltpu.roll(speed[2], LANES - 1, 1), pltpu.roll(speed[2], 1, 1)
    )
    sz = jnp.where((zi == 0) | (zi == 3), 3.0 * jnp.maximum(speed[2], near), 0.0)
    modal = group_transform(u[0], MODAL, 1, zi, 1)
    modal = group_transform(modal, MODAL, 0, yi, 1)
    modal = group_transform(modal, MODAL, 0, xi, 4)
    squares = modal * modal
    edge = jnp.where((zi == 3) | (yi == 3) | (xi == 3), squares, 0.0)
    ones = [[1.0] * 4] * 4
    sums = []
    for s in (squares, edge):
        s = jnp.broadcast_to(jnp.sum(s, axis=0, keepdims=True), (8, LANES))
        sums.append(group_transform(s, ones, 1, zi[:8], 1))
    sensor = jnp.log(sums[1] / sums[0] + 1e-10) * (1.0 / math.log(10.0))
    shape = 1.0 / (1.0 + jnp.exp(-(sensor + 2.3) * 2.0))
    spread = jnp.where(
        lax.broadcasted_iota(jnp.int32, (32, LANES), 1) // 4
        == lax.broadcasted_iota(jnp.int32, (32, LANES), 0),
        1.0,
        0.0,
    )
    element_flags = jnp.broadcast_to(flags_ref[...].astype(jnp.float32), (8, 32))
    flags = jnp.dot(element_flags, spread, preferred_element_type=jnp.float32)
    ahead = jnp.where(
        lax.broadcasted_iota(jnp.int32, (32, LANES), 1) // 4
        > lax.broadcasted_iota(jnp.int32, (32, LANES), 0),
        1.0,
        0.0,
    )
    rank = jnp.dot(element_flags, ahead, preferred_element_type=jnp.float32)
    place = 4.0 * rank + zi[:8].astype(jnp.float32)
    coef_ref[PLACE_AT : PLACE_AT + 8, :] = jnp.where(flags > 0.5, place, -1000.0)
    nu = 0.1 * flags * shape
    nu = jnp.concatenate([nu, nu], axis=0)
    table = {
        V1: v[0], V2: v[1], V3: v[2],
        W1: 0.4 * v[0], W2: 0.4 * v[1], W3: 0.4 * v[2],
        KE: 0.4 * ke, HH: (u[4] + pressure) * inv,
        SX: speed[0], SY: speed[1], SZ: sz, NU: nu,
    }
    for name, value in table.items():
        coef_ref[name * 16 : (name + 1) * 16, :] = value


def selection(place):
    m = lax.broadcasted_iota(jnp.int32, (LANES, LANES), 0).astype(jnp.float32)
    lower = jnp.where(m == place, 1.0, 0.0).astype(jnp.bfloat16)
    upper = jnp.where(m == place + 64.0, 1.0, 0.0).astype(jnp.bfloat16)
    return jnp.concatenate([lower, upper], axis=1)


def select(value, chosen, dims):
    hi = value.astype(jnp.bfloat16)
    lo = (value - hi.astype(jnp.float32)).astype(jnp.bfloat16)
    both = lax.dot_general(
        jnp.concatenate([hi, lo], axis=0),
        chosen,
        (dims, ((), ())),
        preferred_element_type=jnp.float32,
    )
    rows = value.shape[0]
    return both[:rows] + both[rows:]


def wide_at(face, f, n):
    item = f * 4 + n
    r, c = face * HALF + (item % 10) * 8, (item // 10) * LANES
    return slice(r, r + 8), slice(c, c + LANES)


def pack_faces(load, coef_ref, outs, odd_x, odd_y, wide):
    for axis, (near, far), odd in ((0, outs[:2], odd_x), (1, outs[2:], odd_y)):
        for f in range(5):
            for n in range(4):
                line = [load(f, k, n) if axis == 0 else load(f, n, k) for k in range(4)]
                lower = line[0] * DERIV[0][0]
                upper = line[3] * DERIV[3][3]
                for k in range(1, 4):
                    lower = lower + DERIV[0][k] * line[k]
                    upper = upper + DERIV[3][3 - k] * line[3 - k]
                r = face_row(f, n)
                near[r : r + 8, :] = jnp.where(odd, line[0], line[3])
                far[r : r + 8, :] = jnp.where(odd, line[3], line[0])
                wide[wide_at(2 * axis, f, n)] = jnp.where(odd, lower, upper)
                wide[wide_at(2 * axis + 1, f, n)] = jnp.where(odd, upper, lower)
    chosen = selection(coef_ref[PLACE_AT : PLACE_AT + 1, :])
    packed = select(wide[...], chosen, ((1,), (1,)))
    for face in range(4):
        outs[face][FACE:COEF_AT, :] = packed[face * HALF : (face + 1) * HALF]


def by_face(refs, order):
    return tuple(refs[order.index(face)] for face in range(4))


def pack_kernel(t_hbm, base_hbm, flags_hbm, coef_ref, *refs):
    xn, xf, yn, yf = by_face(refs[:4], ORDER_1)
    t_ref, base_ref, flags_ref, wide, sems = refs[4:]
    copies = [
        pltpu.make_async_copy(src, dst, sems.at[k])
        for k, (src, dst) in enumerate(
            ((base_hbm, base_ref), (flags_hbm, flags_ref), (t_hbm, t_ref))
        )
    ]
    for copy in copies:
        copy.start()
    odd_x = lax.axis_index("gx") % 2 == 1
    odd_y = lax.axis_index("gy") % 2 == 1
    copies[0].wait()
    copies[1].wait()
    base_coefs(base_ref, flags_ref, coef_ref)
    copies[2].wait()
    faces = (xn, xf, yn, yf)
    load = lambda f, x, y: tan_in(t_ref, f, x, y)
    pack_faces(load, coef_ref, faces, odd_x, odd_y, wide)
    for axis, (near, far), odd in ((0, (xn, xf), odd_x), (1, (yn, yf), odd_y)):
        for place, name in enumerate(FACE_NAMES + (SX + axis,)):
            first = name * 16
            if axis == 0:
                lower = coef_ref[first : first + 4, :]
                upper = coef_ref[first + 12 : first + 16, :]
            else:
                lower = coef_ref[pl.ds(first, 4, stride=4), :]
                upper = coef_ref[pl.ds(first + 3, 4, stride=4), :]
            r = COEF_AT + 4 * place
            near[r : r + 4, :] = jnp.where(odd, lower, upper)
            far[r : r + 4, :] = jnp.where(odd, upper, lower)
        r = COEF_AT + 28
        near[r : r + 4, :] = coef_ref[PLACE_AT : PLACE_AT + 4, :]
        far[r : r + 4, :] = coef_ref[PLACE_AT : PLACE_AT + 4, :]


def flux(d, t, v, dp, e, hh):
    u = t[1 + d] - v[d] * t[0]
    out = [t[1 + d]]
    for i in range(3):
        value = v[d] * t[1 + i] + v[i] * u
        out.append(value + dp if i == d else value)
    out.append(v[d] * e + hh * u)
    return out


def volume(load, coef_ref, wm_ref, acc, ops, aux):
    top_lane = lax.broadcasted_iota(jnp.int32, (COLS, LANES), 1) % 4 == 3
    chunk = 128

    def put(f, x, y, value):
        hi = value.astype(jnp.bfloat16)
        r = row(f, x, y)
        ops[r : r + 16, :LANES] = hi
        ops[r : r + 16, LANES:] = (value - hi.astype(jnp.float32)).astype(jnp.bfloat16)

    def span_product():
        for c in range(640 // chunk):
            both = jnp.dot(
                ops[c * chunk : (c + 1) * chunk, :],
                wm_ref[...],
                preferred_element_type=jnp.float32,
            )
            acc[c * chunk : (c + 1) * chunk, :] = both[:, :LANES] + both[:, LANES:]

    for x in range(4):
        for f in range(5):
            for y in (0, 2):
                put(f, x, y, jnp.concatenate([load(f, x, y), load(f, x, y + 1)], axis=0))
    span_product()

    for x in range(4):
        for y in (0, 2):
            parts = []
            for yy in (y, y + 1):
                t = [load(f, x, yy) for f in range(5)]
                v = [coef(coef_ref, V1 + d, x, yy) for d in range(3)]
                w = [coef(coef_ref, W1 + d, x, yy) for d in range(3)]
                dp = 0.4 * t[4] + coef(coef_ref, KE, x, yy) * t[0]
                for d in range(3):
                    dp = dp - w[d] * t[1 + d]
                e = t[4] + dp
                k = (x * 4 + yy) * 16
                aux[k : k + 8, :] = dp
                aux[k + 8 : k + 16, :] = e
                g = flux(2, t, v, dp, e, coef(coef_ref, HH, x, yy))
                nu = coef(coef_ref, NU, x, yy)
                out = []
                for f in range(5):
                    r = row(f, x, yy)
                    out.append(nu * acc[r : r + 8, :] - g[f])
                parts.append(out)
            for f in range(5):
                put(f, x, y, jnp.concatenate([parts[0][f], parts[1][f]], axis=0))
    span_product()

    for axis in range(2):
        for n in range(4):
            line = [(k, n) if axis == 0 else (n, k) for k in range(4)]
            t = [[load(f, x, y) for f in range(5)] for x, y in line]
            g = []
            for k, (x, y) in enumerate(line):
                v = [coef(coef_ref, V1 + d, x, y) for d in range(3)]
                r = (x * 4 + y) * 16
                g.append(
                    flux(axis, t[k], v, aux[r : r + 8, :], aux[r + 8 : r + 16, :],
                         coef(coef_ref, HH, x, y))
                )
            nu = coef(coef_ref, NU, *line[0])
            for f in range(5):
                tt = [t[k][f] for k in range(4)]
                fl = []
                for i in range(4):
                    fl.append(nu * row_product(i, tt) - g[i][f])
                for i, (x, y) in enumerate(line):
                    r = row(f, x, y)
                    total = acc[r : r + 8, :] + row_product(i, fl)
                    if axis == 0:
                        other = jnp.where(
                            top_lane, pltpu.roll(tt[i], LANES - 1, 1), pltpu.roll(tt[i], 1, 1)
                        )
                        total = total + coef(coef_ref, SZ, x, y) * (other - tt[i])
                    acc[r : r + 8, :] = total


def row_product(i, values):
    total = None
    for k in range(4):
        if k != i:
            term = DERIV[i][k] * values[k]
            total = term if total is None else total + term
    return total


def add_faces(load, coef_ref, recv, coef_recv, odd_x, odd_y, acc, work, wide, finish):
    for face in range(4):
        r = COEF_AT + 28
        chosen = selection(coef_recv[face][r : r + 1, :])
        wide[face * HALF : (face + 1) * HALF, :] = select(
            recv[face][FACE:COEF_AT, :], chosen, ((1,), (0,))
        )
    for axis, odd in ((0, odd_x), (1, odd_y)):
        near, far = recv[2 * axis : 2 * axis + 2]
        near_c, far_c = coef_recv[2 * axis : 2 * axis + 2]

        def pick(low, r, rows=8):
            a, b = near[r : r + rows, :], far[r : r + rows, :]
            return jnp.where(odd, a, b) if low else jnp.where(odd, b, a)

        def pick_coef(low, place, n):
            r = COEF_AT + 4 * place + n
            a, b = near_c[r : r + 1, :], far_c[r : r + 1, :]
            return jnp.where(odd, a, b) if low else jnp.where(odd, b, a)

        for n in range(4):
            line = [(k, n) if axis == 0 else (n, k) for k in range(4)]
            nu3 = 3.0 * coef(coef_ref, NU, *line[0])
            shift, extra = [], []
            for low in (True, False):
                place = line[0] if low else line[3]
                far_t = [pick(low, face_row(f, n)) for f in range(5)]
                v = [pick_coef(low, d, n) for d in range(3)]
                dp = 0.4 * far_t[4] + pick_coef(low, 3, n) * far_t[0]
                for d in range(3):
                    dp = dp - (0.4 * v[d]) * far_t[1 + d]
                far_g = flux(axis, far_t, v, dp, far_t[4] + dp, pick_coef(low, 4, n))
                far_nu = pick_coef(low, 5, n)
                s3 = 3.0 * jnp.maximum(
                    coef(coef_ref, SX + axis, *place), pick_coef(low, 6, n)
                )
                moved, added = [], []
                for f in range(5):
                    gap = far_t[f] - load(f, *place)
                    a = wide[wide_at(2 * axis, f, n)]
                    b = wide[wide_at(2 * axis + 1, f, n)]
                    far_d = jnp.where(odd, a, b) if low else jnp.where(odd, b, a)
                    far_q = far_d - 3.0 * gap if low else far_d + 3.0 * gap
                    value = 3.0 * (far_nu * far_q - far_g[f])
                    added.append(s3 * gap - value if low else s3 * gap + value)
                    moved.append(-(nu3 * far_t[f]) if low else nu3 * far_t[f])
                shift.append(moved)
                extra.append(added)
            for f in range(5):
                for i, (x, y) in enumerate(line):
                    r = row(f, x, y)
                    total = (acc if axis == 0 else work)[r : r + 8, :]
                    if i != 0:
                        total = total + DERIV[i][0] * shift[0][f]
                    if i != 3:
                        total = total + DERIV[i][3] * shift[1][f]
                    if i == 0:
                        total = total + extra[0][f]
                    if i == 3:
                        total = total + extra[1][f]
                    if axis == 0:
                        work[r : r + 8, :] = total
                    else:
                        finish(f, x, y, total)


def loader(ref):
    def load(f, x, y):
        r = row(f, x, y)
        return ref[r : r + 8, :]

    return load


def first_volume(t_ref, coef_ref, acc, wm_ref, ops, aux):
    span_table(wm_ref)
    volume(lambda f, x, y: tan_in(t_ref, f, x, y), coef_ref, wm_ref, acc, ops, aux)


def second_volume(s_ref, coef_ref, wm_ref, acc, ops, aux):
    volume(loader(s_ref), coef_ref, wm_ref, acc, ops, aux)


def first_faces(t_ref, coef_ref, acc, r0, r1, r2, r3, s_ref, m0, m1, m2, m3, work, wide):
    odd_x = lax.axis_index("gx") % 2 == 1
    odd_y = lax.axis_index("gy") % 2 == 1
    load = lambda f, x, y: tan_in(t_ref, f, x, y)

    def finish(f, x, y, total):
        r = row(f, x, y)
        s_ref[r : r + 8, :] = load(f, x, y) + STEP * total

    faces = by_face((r0, r1, r2, r3), ORDER_1)
    add_faces(load, coef_ref, faces, faces, odd_x, odd_y, acc, work, wide, finish)
    sent = by_face((m0, m1, m2, m3), ORDER_2)
    pack_faces(loader(s_ref), coef_ref, sent, odd_x, odd_y, wide)


def second_faces(
    t_ref, s_ref, coef_ref, acc, c0, c1, c2, c3, r0, r1, r2, r3, out_ref, work, wide
):
    odd_x = lax.axis_index("gx") % 2 == 1
    odd_y = lax.axis_index("gy") % 2 == 1
    load = loader(s_ref)

    def finish(f, x, y, total):
        value = 0.5 * tan_in(t_ref, f, x, y) + (0.5 * load(f, x, y) + (0.5 * STEP) * total)
        out_ref[pl.ds(f * 16 + x * 4 + y, COLS, stride=80), :] = value

    add_faces(
        load, coef_ref, by_face((r0, r1, r2, r3), ORDER_2),
        by_face((c0, c1, c2, c3), ORDER_1), odd_x, odd_y, acc, work, wide, finish,
    )


def call(kernel, shapes, scratch, args, flops, space=pltpu.VMEM, limit=16):
    return pl.pallas_call(
        kernel,
        out_shape=[
            s if hasattr(s, "dtype") else jax.ShapeDtypeStruct(s, jnp.float32) for s in shapes
        ],
        in_specs=[pl.BlockSpec(memory_space=space)] * len(args),
        out_specs=[pl.BlockSpec(memory_space=pltpu.VMEM)] * len(shapes),
        scratch_shapes=scratch,
        compiler_params=pltpu.CompilerParams(vmem_limit_bytes=limit * 1024 * 1024),
        cost_estimate=pl.CostEstimate(flops=flops, bytes_accessed=1000000, transcendentals=0),
    )(*args)


def exchange(messages, order):
    size_x, size_y = lax.axis_size("gx"), lax.axis_size("gy")

    def pairs(size, first):
        out = []
        for i in range(first, size - 1, 2):
            out += [(i, i + 1), (i + 1, i)]
        if first == 1:
            out += [(0, 0)]
            if size % 2 == 0:
                out += [(size - 1, size - 1)]
        return out

    plan = (
        ("gx", pairs(size_x, 0)),
        ("gx", pairs(size_x, 1)),
        ("gy", pairs(size_y, 0)),
        ("gy", pairs(size_y, 1)),
    )
    return [lax.ppermute(m, *plan[face]) for m, face in zip(messages, order)]


def per_device(tangent, base_state, shock_flags):
    t = tangent.reshape(640, LANES)
    base = base_state.reshape(80, LANES)
    flags = shock_flags.reshape(1, 32)
    message = (COEF_AT + COEF_ROWS, LANES)
    short = (COEF_AT, LANES)
    whole = (640, LANES)
    volume_scratch = [
        pltpu.VMEM((640, 2 * LANES), jnp.bfloat16),
        pltpu.VMEM((256, LANES), jnp.float32),
    ]
    wide = pltpu.VMEM((4 * HALF, 2 * LANES), jnp.float32)
    work = [pltpu.VMEM(whole, jnp.float32), wide]
    staging = [
        pltpu.VMEM(whole, jnp.float32),
        pltpu.VMEM(base.shape, jnp.float32),
        pltpu.VMEM(flags.shape, jnp.int32),
        wide,
        pltpu.SemaphoreType.DMA((3,)),
    ]
    coefs, *faces = call(
        pack_kernel, [(PLACE_AT + 8, LANES)] + [message] * 4, staging, [t, base, flags], 1000000,
        space=pltpu.HBM, limit=56,
    )
    got = exchange(faces, ORDER_1)
    inner, wm = call(
        first_volume, [whole, jax.ShapeDtypeStruct((256, 256), jnp.bfloat16)], volume_scratch, [t, coefs],
        10000000,
    )
    s, *faces = call(
        first_faces, [whole] + [short] * 4, work, [t, coefs, inner, *got], 1000000
    )
    again = exchange(faces, ORDER_2)
    (inner,) = call(second_volume, [whole], volume_scratch, [s, coefs, wm], 10000000)
    (out,) = call(second_faces, [whole], work, [t, s, coefs, inner, *got, *again], 1000000)
    return out.reshape(tangent.shape)


def solution(mesh):
    in_specs = (P(None, None, "gx", "gy", None), P(None, "gx", "gy", None), P("gx", "gy", None))
    out_specs = P(None, None, "gx", "gy", None)
    return jax.shard_map(
        per_device, mesh=mesh, in_specs=in_specs, out_specs=out_specs, check_vma=False
    )
```

```python
import math

import jax
import jax.numpy as jnp
import numpy as np
from jax import lax
from jax.experimental import pallas as pl
from jax.experimental.pallas import tpu as pltpu
from jax.sharding import PartitionSpec as P

STEP = 0.1
COLS = 8
LANES = 128
V1, V2, V3, W1, W2, W3, KE, HH, SX, SY, SZ, NU = range(12)
FACE = 160
HALF = 80
FACE_NAMES = (V1, V2, V3, KE, HH, NU)
COEF_ROWS = 32
COEF_AT = FACE + HALF
PLACE_AT = 12 * 16
ORDER_1 = (1, 3, 0, 2)
ORDER_2 = (1, 3, 0, 2)


def node_tables():
    inner_point = math.sqrt(0.2)
    points = [-1.0, -inner_point, inner_point, 1.0]
    weights = [1.0 / 6.0, 5.0 / 6.0, 5.0 / 6.0, 1.0 / 6.0]
    barycentric = []
    for j in range(4):
        product = 1.0
        for k in range(4):
            if k != j:
                product = product * (points[j] - points[k])
        barycentric.append(1.0 / product)
    deriv = [[0.0] * 4 for i in range(4)]
    for i in range(4):
        for j in range(4):
            if j != i:
                deriv[i][j] = barycentric[j] / barycentric[i] / (points[i] - points[j])
        deriv[i][i] = -sum((deriv[i][j] for j in range(4) if j != i))
    norms = [2.0, 2.0 / 3.0, 2.0 / 5.0, 2.0 / 3.0]
    legendre = [
        lambda x: 1.0,
        lambda x: x,
        lambda x: 0.5 * (3.0 * x * x - 1.0),
        lambda x: 0.5 * (5.0 * x * x * x - 3.0 * x),
    ]
    modal = [[weights[i] * legendre[k](points[i]) / norms[k] for i in range(4)] for k in range(4)]
    return deriv, modal


DERIV, MODAL = node_tables()


def span_table(wm_ref):
    k = lax.broadcasted_iota(jnp.int32, (LANES, LANES), 0)
    n = lax.broadcasted_iota(jnp.int32, (LANES, LANES), 1)
    place = (n % 4) * LANES + ((k - n) & (LANES - 1))
    hi = jnp.zeros((LANES, LANES), jnp.float32)
    lo = hi
    entries = [(i, j - i, DERIV[i][j]) for i in range(4) for j in range(4) if i != j]
    for i, offset, value in entries + [(0, -1, -3.0), (3, 1, 3.0)]:
        head = float(np.float32(value).astype(jnp.bfloat16))
        here = place == i * LANES + (offset & (LANES - 1))
        hi = jnp.where(here, head, hi)
        lo = jnp.where(here, value - head, lo)
    hi, lo = hi.astype(jnp.bfloat16), lo.astype(jnp.bfloat16)
    wm_ref[:LANES, :LANES] = hi
    wm_ref[LANES:, :LANES] = hi
    wm_ref[:LANES, LANES:] = lo
    wm_ref[LANES:, LANES:] = jnp.zeros_like(lo)


def row(f, x, y):
    return (f * 16 + x * 4 + y) * COLS


def face_row(f, n):
    return (f * 4 + n) * COLS


def tan_in(ref, f, x, y):
    return ref[pl.ds(f * 16 + x * 4 + y, COLS, stride=80), :]


def coef(ref, name, x, y):
    r = name * 16 + x * 4 + y
    return ref[r : r + 1, :]


def group_transform(f, matrix, axis, index, step):
    size = f.shape[axis]
    total = None
    for offset in range(-3, 4):
        c = jnp.zeros_like(f)
        for i in range(4):
            if 0 <= i + offset < 4:
                c = jnp.where(index == i, matrix[i][i + offset], c)
        moved = f if offset == 0 else pltpu.roll(f, (-offset * step) % size, axis)
        term = c * moved
        total = term if total is None else total + term
    return total


def base_coefs(base_ref, flags_ref, coef_ref):
    u = [base_ref[f * 16 : (f + 1) * 16, :] for f in range(5)]
    inv = 1.0 / u[0]
    v = [u[1 + d] * inv for d in range(3)]
    ke = 0.5 * (v[0] * v[0] + v[1] * v[1] + v[2] * v[2])
    pressure = 0.4 * (u[4] - ke * u[0])
    sound = jnp.sqrt(1.4 * pressure * inv)
    speed = [jnp.abs(v[d]) + sound for d in range(3)]
    lane = lax.broadcasted_iota(jnp.int32, (16, LANES), 1)
    sub = lax.broadcasted_iota(jnp.int32, (16, LANES), 0)
    zi, yi, xi = lane % 4, sub % 4, sub // 4
    near = jnp.where(
        zi == 3, pltpu.roll(speed[2], LANES - 1, 1), pltpu.roll(speed[2], 1, 1)
    )
    sz = jnp.where((zi == 0) | (zi == 3), 3.0 * jnp.maximum(speed[2], near), 0.0)
    modal = group_transform(u[0], MODAL, 1, zi, 1)
    modal = group_transform(modal, MODAL, 0, yi, 1)
    modal = group_transform(modal, MODAL, 0, xi, 4)
    squares = modal * modal
    edge = jnp.where((zi == 3) | (yi == 3) | (xi == 3), squares, 0.0)
    ones = [[1.0] * 4] * 4
    sums = []
    for s in (squares, edge):
        s = jnp.broadcast_to(jnp.sum(s, axis=0, keepdims=True), (8, LANES))
        sums.append(group_transform(s, ones, 1, zi[:8], 1))
    sensor = jnp.log(sums[1] / sums[0] + 1e-10) * (1.0 / math.log(10.0))
    shape = 1.0 / (1.0 + jnp.exp(-(sensor + 2.3) * 2.0))
    spread = jnp.where(
        lax.broadcasted_iota(jnp.int32, (32, LANES), 1) // 4
        == lax.broadcasted_iota(jnp.int32, (32, LANES), 0),
        1.0,
        0.0,
    )
    element_flags = jnp.broadcast_to(flags_ref[...].astype(jnp.float32), (8, 32))
    flags = jnp.dot(element_flags, spread, preferred_element_type=jnp.float32)
    ahead = jnp.where(
        lax.broadcasted_iota(jnp.int32, (32, LANES), 1) // 4
        > lax.broadcasted_iota(jnp.int32, (32, LANES), 0),
        1.0,
        0.0,
    )
    rank = jnp.dot(element_flags, ahead, preferred_element_type=jnp.float32)
    place = 4.0 * rank + zi[:8].astype(jnp.float32)
    coef_ref[PLACE_AT : PLACE_AT + 8, :] = jnp.where(flags > 0.5, place, -1000.0)
    nu = 0.1 * flags * shape
    nu = jnp.concatenate([nu, nu], axis=0)
    table = {
        V1: v[0], V2: v[1], V3: v[2],
        W1: 0.4 * v[0], W2: 0.4 * v[1], W3: 0.4 * v[2],
        KE: 0.4 * ke, HH: (u[4] + pressure) * inv,
        SX: speed[0], SY: speed[1], SZ: sz, NU: nu,
    }
    for name, value in table.items():
        coef_ref[name * 16 : (name + 1) * 16, :] = value


def selection(place):
    m = lax.broadcasted_iota(jnp.int32, (LANES, LANES), 0).astype(jnp.float32)
    lower = jnp.where(m == place, 1.0, 0.0).astype(jnp.bfloat16)
    upper = jnp.where(m == place + 64.0, 1.0, 0.0).astype(jnp.bfloat16)
    return jnp.concatenate([lower, upper], axis=1)


def select(value, chosen, dims):
    hi = value.astype(jnp.bfloat16)
    lo = (value - hi.astype(jnp.float32)).astype(jnp.bfloat16)
    both = lax.dot_general(
        jnp.concatenate([hi, lo], axis=0),
        chosen,
        (dims, ((), ())),
        preferred_element_type=jnp.float32,
    )
    rows = value.shape[0]
    return both[:rows] + both[rows:]


def wide_at(face, f, n):
    item = f * 4 + n
    r, c = face * HALF + (item % 10) * 8, (item // 10) * LANES
    return slice(r, r + 8), slice(c, c + LANES)


def pack_faces(load, coef_ref, outs, odd_x, odd_y, wide):
    for axis, (near, far), odd in ((0, outs[:2], odd_x), (1, outs[2:], odd_y)):
        for f in range(5):
            for n in range(4):
                line = [load(f, k, n) if axis == 0 else load(f, n, k) for k in range(4)]
                lower = line[0] * DERIV[0][0]
                upper = line[3] * DERIV[3][3]
                for k in range(1, 4):
                    lower = lower + DERIV[0][k] * line[k]
                    upper = upper + DERIV[3][3 - k] * line[3 - k]
                r = face_row(f, n)
                near[r : r + 8, :] = jnp.where(odd, line[0], line[3])
                far[r : r + 8, :] = jnp.where(odd, line[3], line[0])
                wide[wide_at(2 * axis, f, n)] = jnp.where(odd, lower, upper)
                wide[wide_at(2 * axis + 1, f, n)] = jnp.where(odd, upper, lower)
    chosen = selection(coef_ref[PLACE_AT : PLACE_AT + 1, :])
    packed = select(wide[...], chosen, ((1,), (1,)))
    for face in range(4):
        outs[face][FACE:COEF_AT, :] = packed[face * HALF : (face + 1) * HALF]


def by_face(refs, order):
    return tuple(refs[order.index(face)] for face in range(4))


def pack_kernel(t_hbm, base_hbm, flags_hbm, coef_ref, *refs):
    xn, xf, yn, yf = by_face(refs[:4], ORDER_1)
    t_ref, base_ref, flags_ref, wide, sems = refs[4:]
    copies = [
        pltpu.make_async_copy(src, dst, sems.at[k])
        for k, (src, dst) in enumerate(
            ((base_hbm, base_ref), (flags_hbm, flags_ref), (t_hbm, t_ref))
        )
    ]
    for copy in copies:
        copy.start()
    odd_x = lax.axis_index("gx") % 2 == 1
    odd_y = lax.axis_index("gy") % 2 == 1
    copies[0].wait()
    copies[1].wait()
    base_coefs(base_ref, flags_ref, coef_ref)
    copies[2].wait()
    faces = (xn, xf, yn, yf)
    load = lambda f, x, y: tan_in(t_ref, f, x, y)
    pack_faces(load, coef_ref, faces, odd_x, odd_y, wide)
    for axis, (near, far), odd in ((0, (xn, xf), odd_x), (1, (yn, yf), odd_y)):
        for place, name in enumerate(FACE_NAMES + (SX + axis,)):
            first = name * 16
            if axis == 0:
                lower = coef_ref[first : first + 4, :]
                upper = coef_ref[first + 12 : first + 16, :]
            else:
                lower = coef_ref[pl.ds(first, 4, stride=4), :]
                upper = coef_ref[pl.ds(first + 3, 4, stride=4), :]
            r = COEF_AT + 4 * place
            near[r : r + 4, :] = jnp.where(odd, lower, upper)
            far[r : r + 4, :] = jnp.where(odd, upper, lower)
        r = COEF_AT + 28
        near[r : r + 4, :] = coef_ref[PLACE_AT : PLACE_AT + 4, :]
        far[r : r + 4, :] = coef_ref[PLACE_AT : PLACE_AT + 4, :]


def flux(d, t, v, dp, e, hh):
    u = t[1 + d] - v[d] * t[0]
    out = [t[1 + d]]
    for i in range(3):
        value = v[d] * t[1 + i] + v[i] * u
        out.append(value + dp if i == d else value)
    out.append(v[d] * e + hh * u)
    return out


def volume(load, coef_ref, wm_ref, acc, ops, aux, result):
    top_lane = lax.broadcasted_iota(jnp.int32, (COLS, LANES), 1) % 4 == 3
    chunk = 128

    def put(f, x, y, value):
        hi = value.astype(jnp.bfloat16)
        r = row(f, x, y)
        ops[r : r + 16, :LANES] = hi
        ops[r : r + 16, LANES:] = (value - hi.astype(jnp.float32)).astype(jnp.bfloat16)

    def span_product():
        for c in range(640 // chunk):
            both = jnp.dot(
                ops[c * chunk : (c + 1) * chunk, :],
                wm_ref[...],
                preferred_element_type=jnp.float32,
            )
            acc[c * chunk : (c + 1) * chunk, :] = both[:, :LANES] + both[:, LANES:]

    for x in range(4):
        for f in range(5):
            for y in (0, 2):
                put(f, x, y, jnp.concatenate([load(f, x, y), load(f, x, y + 1)], axis=0))
    span_product()

    for x in range(4):
        for y in (0, 2):
            parts = []
            for yy in (y, y + 1):
                t = [load(f, x, yy) for f in range(5)]
                v = [coef(coef_ref, V1 + d, x, yy) for d in range(3)]
                w = [coef(coef_ref, W1 + d, x, yy) for d in range(3)]
                dp = 0.4 * t[4] + coef(coef_ref, KE, x, yy) * t[0]
                for d in range(3):
                    dp = dp - w[d] * t[1 + d]
                e = t[4] + dp
                k = (x * 4 + yy) * 16
                aux[k : k + 8, :] = dp
                aux[k + 8 : k + 16, :] = e
                g = flux(2, t, v, dp, e, coef(coef_ref, HH, x, yy))
                nu = coef(coef_ref, NU, x, yy)
                out = []
                for f in range(5):
                    r = row(f, x, yy)
                    out.append(nu * acc[r : r + 8, :] - g[f])
                parts.append(out)
            for f in range(5):
                put(f, x, y, jnp.concatenate([parts[0][f], parts[1][f]], axis=0))
    span_product()

    for axis in range(2):
        for n in range(4):
            line = [(k, n) if axis == 0 else (n, k) for k in range(4)]
            t = [[load(f, x, y) for f in range(5)] for x, y in line]
            g = []
            for k, (x, y) in enumerate(line):
                v = [coef(coef_ref, V1 + d, x, y) for d in range(3)]
                r = (x * 4 + y) * 16
                g.append(
                    flux(axis, t[k], v, aux[r : r + 8, :], aux[r + 8 : r + 16, :],
                         coef(coef_ref, HH, x, y))
                )
            nu = coef(coef_ref, NU, *line[0])
            for f in range(5):
                tt = [t[k][f] for k in range(4)]
                fl = []
                for i in range(4):
                    fl.append(nu * row_product(i, tt) - g[i][f])
                for i, (x, y) in enumerate(line):
                    r = row(f, x, y)
                    total = acc[r : r + 8, :] + row_product(i, fl)
                    if axis == 0:
                        other = jnp.where(
                            top_lane, pltpu.roll(tt[i], LANES - 1, 1), pltpu.roll(tt[i], 1, 1)
                        )
                        total = total + coef(coef_ref, SZ, x, y) * (other - tt[i])
                    else:
                        total = result(f, x, y, tt[i], total)
                    acc[r : r + 8, :] = total


def row_product(i, values):
    total = None
    for k in range(4):
        if k != i:
            term = DERIV[i][k] * values[k]
            total = term if total is None else total + term
    return total


def add_faces(load, coef_ref, recv, coef_recv, odd_x, odd_y, acc, work, wide, scale, finish):
    for face in range(4):
        r = COEF_AT + 28
        chosen = selection(coef_recv[face][r : r + 1, :])
        wide[face * HALF : (face + 1) * HALF, :] = select(
            recv[face][FACE:COEF_AT, :], chosen, ((1,), (0,))
        )
    for axis, odd in ((0, odd_x), (1, odd_y)):
        near, far = recv[2 * axis : 2 * axis + 2]
        near_c, far_c = coef_recv[2 * axis : 2 * axis + 2]

        def pick(low, r, rows=8):
            a, b = near[r : r + rows, :], far[r : r + rows, :]
            return jnp.where(odd, a, b) if low else jnp.where(odd, b, a)

        def pick_coef(low, place, n):
            r = COEF_AT + 4 * place + n
            a, b = near_c[r : r + 1, :], far_c[r : r + 1, :]
            return jnp.where(odd, a, b) if low else jnp.where(odd, b, a)

        for n in range(4):
            line = [(k, n) if axis == 0 else (n, k) for k in range(4)]
            nu3 = (3.0 * scale) * coef(coef_ref, NU, *line[0])
            shift, extra = [], []
            for low in (True, False):
                place = line[0] if low else line[3]
                far_t = [pick(low, face_row(f, n)) for f in range(5)]
                v = [pick_coef(low, d, n) for d in range(3)]
                dp = 0.4 * far_t[4] + pick_coef(low, 3, n) * far_t[0]
                for d in range(3):
                    dp = dp - (0.4 * v[d]) * far_t[1 + d]
                far_g = flux(axis, far_t, v, dp, far_t[4] + dp, pick_coef(low, 4, n))
                far_nu = pick_coef(low, 5, n)
                s3 = (3.0 * scale) * jnp.maximum(
                    coef(coef_ref, SX + axis, *place), pick_coef(low, 6, n)
                )
                moved, added = [], []
                for f in range(5):
                    gap = far_t[f] - load(f, *place)
                    a = wide[wide_at(2 * axis, f, n)]
                    b = wide[wide_at(2 * axis + 1, f, n)]
                    far_d = jnp.where(odd, a, b) if low else jnp.where(odd, b, a)
                    far_q = far_d - 3.0 * gap if low else far_d + 3.0 * gap
                    value = (3.0 * scale) * (far_nu * far_q - far_g[f])
                    added.append(s3 * gap - value if low else s3 * gap + value)
                    moved.append(-(nu3 * far_t[f]) if low else nu3 * far_t[f])
                shift.append(moved)
                extra.append(added)
            for f in range(5):
                for i, (x, y) in enumerate(line):
                    r = row(f, x, y)
                    total = (acc if axis == 0 else work)[r : r + 8, :]
                    if i != 0:
                        total = total + DERIV[i][0] * shift[0][f]
                    if i != 3:
                        total = total + DERIV[i][3] * shift[1][f]
                    if i == 0:
                        total = total + extra[0][f]
                    if i == 3:
                        total = total + extra[1][f]
                    if axis == 0:
                        work[r : r + 8, :] = total
                    else:
                        finish(f, x, y, total)


def loader(ref):
    def load(f, x, y):
        r = row(f, x, y)
        return ref[r : r + 8, :]

    return load


def first_volume(t_ref, coef_ref, acc, wm_ref, ops, aux):
    span_table(wm_ref)
    volume(
        lambda f, x, y: tan_in(t_ref, f, x, y), coef_ref, wm_ref, acc, ops, aux,
        lambda f, x, y, t, total: t + STEP * total,
    )


def second_volume(t_ref, s_ref, coef_ref, wm_ref, acc, ops, aux):
    def result(f, x, y, s, total):
        return 0.5 * tan_in(t_ref, f, x, y) + (0.5 * s + (0.5 * STEP) * total)

    volume(loader(s_ref), coef_ref, wm_ref, acc, ops, aux, result)


def first_faces(t_ref, coef_ref, acc, r0, r1, r2, r3, s_ref, m0, m1, m2, m3, work, wide):
    odd_x = lax.axis_index("gx") % 2 == 1
    odd_y = lax.axis_index("gy") % 2 == 1
    load = lambda f, x, y: tan_in(t_ref, f, x, y)

    def finish(f, x, y, total):
        r = row(f, x, y)
        s_ref[r : r + 8, :] = total

    faces = by_face((r0, r1, r2, r3), ORDER_1)
    add_faces(load, coef_ref, faces, faces, odd_x, odd_y, acc, work, wide, STEP, finish)
    sent = by_face((m0, m1, m2, m3), ORDER_2)
    pack_faces(loader(s_ref), coef_ref, sent, odd_x, odd_y, wide)


def second_faces(
    s_ref, coef_ref, acc, c0, c1, c2, c3, r0, r1, r2, r3, out_ref, work, wide
):
    odd_x = lax.axis_index("gx") % 2 == 1
    odd_y = lax.axis_index("gy") % 2 == 1
    load = loader(s_ref)

    def finish(f, x, y, total):
        out_ref[pl.ds(f * 16 + x * 4 + y, COLS, stride=80), :] = total

    add_faces(
        load, coef_ref, by_face((r0, r1, r2, r3), ORDER_2),
        by_face((c0, c1, c2, c3), ORDER_1), odd_x, odd_y, acc, work, wide, 0.5 * STEP, finish,
    )


def call(kernel, shapes, scratch, args, flops, space=pltpu.VMEM, limit=16):
    return pl.pallas_call(
        kernel,
        out_shape=[
            s if hasattr(s, "dtype") else jax.ShapeDtypeStruct(s, jnp.float32) for s in shapes
        ],
        in_specs=[pl.BlockSpec(memory_space=space)] * len(args),
        out_specs=[pl.BlockSpec(memory_space=pltpu.VMEM)] * len(shapes),
        scratch_shapes=scratch,
        compiler_params=pltpu.CompilerParams(vmem_limit_bytes=limit * 1024 * 1024),
        cost_estimate=pl.CostEstimate(flops=flops, bytes_accessed=1000000, transcendentals=0),
    )(*args)


def exchange(messages, order):
    size_x, size_y = lax.axis_size("gx"), lax.axis_size("gy")

    def pairs(size, first):
        out = []
        for i in range(first, size - 1, 2):
            out += [(i, i + 1), (i + 1, i)]
        if first == 1:
            out += [(0, 0)]
            if size % 2 == 0:
                out += [(size - 1, size - 1)]
        return out

    plan = (
        ("gx", pairs(size_x, 0)),
        ("gx", pairs(size_x, 1)),
        ("gy", pairs(size_y, 0)),
        ("gy", pairs(size_y, 1)),
    )
    return [lax.ppermute(m, *plan[face]) for m, face in zip(messages, order)]


def per_device(tangent, base_state, shock_flags):
    t = tangent.reshape(640, LANES)
    base = base_state.reshape(80, LANES)
    flags = shock_flags.reshape(1, 32)
    message = (COEF_AT + COEF_ROWS, LANES)
    short = (COEF_AT, LANES)
    whole = (640, LANES)
    volume_scratch = [
        pltpu.VMEM((640, 2 * LANES), jnp.bfloat16),
        pltpu.VMEM((256, LANES), jnp.float32),
    ]
    wide = pltpu.VMEM((4 * HALF, 2 * LANES), jnp.float32)
    work = [pltpu.VMEM(whole, jnp.float32), wide]
    staging = [
        pltpu.VMEM(whole, jnp.float32),
        pltpu.VMEM(base.shape, jnp.float32),
        pltpu.VMEM(flags.shape, jnp.int32),
        wide,
        pltpu.SemaphoreType.DMA((3,)),
    ]
    coefs, *faces = call(
        pack_kernel, [(PLACE_AT + 8, LANES)] + [message] * 4, staging, [t, base, flags], 1000000,
        space=pltpu.HBM, limit=56,
    )
    got = exchange(faces, ORDER_1)
    inner, wm = call(
        first_volume, [whole, jax.ShapeDtypeStruct((256, 256), jnp.bfloat16)], volume_scratch, [t, coefs],
        10000000,
    )
    s, *faces = call(
        first_faces, [whole] + [short] * 4, work, [t, coefs, inner, *got], 1000000
    )
    again = exchange(faces, ORDER_2)
    (inner,) = call(second_volume, [whole], volume_scratch, [t, s, coefs, wm], 10000000)
    (out,) = call(second_faces, [whole], work, [s, coefs, inner, *got, *again], 1000000)
    return out.reshape(tangent.shape)


def solution(mesh):
    in_specs = (P(None, None, "gx", "gy", None), P(None, "gx", "gy", None), P("gx", "gy", None))
    out_specs = P(None, None, "gx", "gy", None)
    return jax.shard_map(
        per_device, mesh=mesh, in_specs=in_specs, out_specs=out_specs, check_vma=False
    )
```

```python
import math

import jax
import jax.numpy as jnp
import numpy as np
from jax import lax
from jax.experimental import pallas as pl
from jax.experimental.pallas import tpu as pltpu
from jax.sharding import PartitionSpec as P

STEP = 0.1
COLS = 8
LANES = 128
V1, V2, V3, W1, W2, W3, KE, HH, SX, SY, SZ, NU = range(12)
FACE = 160
HALF = 80
FACE_NAMES = (V1, V2, V3, KE, HH, NU)
COEF_ROWS = 32
COEF_AT = FACE + HALF
PLACE_AT = 12 * 16
ORDER_1 = (0, 1, 3, 2)
ORDER_2 = (1, 3, 0, 2)


def node_tables():
    inner_point = math.sqrt(0.2)
    points = [-1.0, -inner_point, inner_point, 1.0]
    weights = [1.0 / 6.0, 5.0 / 6.0, 5.0 / 6.0, 1.0 / 6.0]
    barycentric = []
    for j in range(4):
        product = 1.0
        for k in range(4):
            if k != j:
                product = product * (points[j] - points[k])
        barycentric.append(1.0 / product)
    deriv = [[0.0] * 4 for i in range(4)]
    for i in range(4):
        for j in range(4):
            if j != i:
                deriv[i][j] = barycentric[j] / barycentric[i] / (points[i] - points[j])
        deriv[i][i] = -sum((deriv[i][j] for j in range(4) if j != i))
    norms = [2.0, 2.0 / 3.0, 2.0 / 5.0, 2.0 / 3.0]
    legendre = [
        lambda x: 1.0,
        lambda x: x,
        lambda x: 0.5 * (3.0 * x * x - 1.0),
        lambda x: 0.5 * (5.0 * x * x * x - 3.0 * x),
    ]
    modal = [[weights[i] * legendre[k](points[i]) / norms[k] for i in range(4)] for k in range(4)]
    return deriv, modal


DERIV, MODAL = node_tables()


def span_table(wm_ref):
    k = lax.broadcasted_iota(jnp.int32, (LANES, LANES), 0)
    n = lax.broadcasted_iota(jnp.int32, (LANES, LANES), 1)
    place = (n % 4) * LANES + ((k - n) & (LANES - 1))
    hi = jnp.zeros((LANES, LANES), jnp.float32)
    lo = hi
    entries = [(i, j - i, DERIV[i][j]) for i in range(4) for j in range(4) if i != j]
    for i, offset, value in entries + [(0, -1, -3.0), (3, 1, 3.0)]:
        head = float(np.float32(value).astype(jnp.bfloat16))
        here = place == i * LANES + (offset & (LANES - 1))
        hi = jnp.where(here, head, hi)
        lo = jnp.where(here, value - head, lo)
    hi, lo = hi.astype(jnp.bfloat16), lo.astype(jnp.bfloat16)
    wm_ref[:LANES, :LANES] = hi
    wm_ref[LANES:, :LANES] = hi
    wm_ref[:LANES, LANES:] = lo
    wm_ref[LANES:, LANES:] = jnp.zeros_like(lo)


def row(f, x, y):
    return (f * 16 + x * 4 + y) * COLS


def face_row(f, n):
    return (f * 4 + n) * COLS


def tan_in(ref, f, x, y):
    return ref[pl.ds(f * 16 + x * 4 + y, COLS, stride=80), :]


def coef(ref, name, x, y):
    r = name * 16 + x * 4 + y
    return ref[r : r + 1, :]


def group_transform(f, matrix, axis, index, step):
    size = f.shape[axis]
    total = None
    for offset in range(-3, 4):
        c = jnp.zeros_like(f)
        for i in range(4):
            if 0 <= i + offset < 4:
                c = jnp.where(index == i, matrix[i][i + offset], c)
        moved = f if offset == 0 else pltpu.roll(f, (-offset * step) % size, axis)
        term = c * moved
        total = term if total is None else total + term
    return total


def base_coefs(base_ref, flags_ref, coef_ref):
    u = [base_ref[f * 16 : (f + 1) * 16, :] for f in range(5)]
    inv = 1.0 / u[0]
    v = [u[1 + d] * inv for d in range(3)]
    ke = 0.5 * (v[0] * v[0] + v[1] * v[1] + v[2] * v[2])
    pressure = 0.4 * (u[4] - ke * u[0])
    sound = jnp.sqrt(1.4 * pressure * inv)
    speed = [jnp.abs(v[d]) + sound for d in range(3)]
    lane = lax.broadcasted_iota(jnp.int32, (16, LANES), 1)
    sub = lax.broadcasted_iota(jnp.int32, (16, LANES), 0)
    zi, yi, xi = lane % 4, sub % 4, sub // 4
    near = jnp.where(
        zi == 3, pltpu.roll(speed[2], LANES - 1, 1), pltpu.roll(speed[2], 1, 1)
    )
    sz = jnp.where((zi == 0) | (zi == 3), 3.0 * jnp.maximum(speed[2], near), 0.0)
    modal = group_transform(u[0], MODAL, 1, zi, 1)
    modal = group_transform(modal, MODAL, 0, yi, 1)
    modal = group_transform(modal, MODAL, 0, xi, 4)
    squares = modal * modal
    edge = jnp.where((zi == 3) | (yi == 3) | (xi == 3), squares, 0.0)
    ones = [[1.0] * 4] * 4
    sums = []
    for s in (squares, edge):
        s = jnp.broadcast_to(jnp.sum(s, axis=0, keepdims=True), (8, LANES))
        sums.append(group_transform(s, ones, 1, zi[:8], 1))
    sensor = jnp.log(sums[1] / sums[0] + 1e-10) * (1.0 / math.log(10.0))
    shape = 1.0 / (1.0 + jnp.exp(-(sensor + 2.3) * 2.0))
    spread = jnp.where(
        lax.broadcasted_iota(jnp.int32, (32, LANES), 1) // 4
        == lax.broadcasted_iota(jnp.int32, (32, LANES), 0),
        1.0,
        0.0,
    )
    element_flags = jnp.broadcast_to(flags_ref[...].astype(jnp.float32), (8, 32))
    flags = jnp.dot(element_flags, spread, preferred_element_type=jnp.float32)
    ahead = jnp.where(
        lax.broadcasted_iota(jnp.int32, (32, LANES), 1) // 4
        > lax.broadcasted_iota(jnp.int32, (32, LANES), 0),
        1.0,
        0.0,
    )
    rank = jnp.dot(element_flags, ahead, preferred_element_type=jnp.float32)
    place = 4.0 * rank + zi[:8].astype(jnp.float32)
    coef_ref[PLACE_AT : PLACE_AT + 8, :] = jnp.where(flags > 0.5, place, -1000.0)
    nu = 0.1 * flags * shape
    nu = jnp.concatenate([nu, nu], axis=0)
    table = {
        V1: v[0], V2: v[1], V3: v[2],
        W1: 0.4 * v[0], W2: 0.4 * v[1], W3: 0.4 * v[2],
        KE: 0.4 * ke, HH: (u[4] + pressure) * inv,
        SX: speed[0], SY: speed[1], SZ: sz, NU: nu,
    }
    for name, value in table.items():
        coef_ref[name * 16 : (name + 1) * 16, :] = value


def selection(place):
    m = lax.broadcasted_iota(jnp.int32, (LANES, LANES), 0).astype(jnp.float32)
    lower = jnp.where(m == place, 1.0, 0.0).astype(jnp.bfloat16)
    upper = jnp.where(m == place + 64.0, 1.0, 0.0).astype(jnp.bfloat16)
    return jnp.concatenate([lower, upper], axis=1)


def select(value, chosen, dims):
    hi = value.astype(jnp.bfloat16)
    lo = (value - hi.astype(jnp.float32)).astype(jnp.bfloat16)
    both = lax.dot_general(
        jnp.concatenate([hi, lo], axis=0),
        chosen,
        (dims, ((), ())),
        preferred_element_type=jnp.float32,
    )
    rows = value.shape[0]
    return both[:rows] + both[rows:]


def wide_at(face, f, n):
    item = f * 4 + n
    r, c = face * HALF + (item % 10) * 8, (item // 10) * LANES
    return slice(r, r + 8), slice(c, c + LANES)


def pack_faces(load, coef_ref, outs, odd_x, odd_y, wide):
    for axis, (near, far), odd in ((0, outs[:2], odd_x), (1, outs[2:], odd_y)):
        for f in range(5):
            for n in range(4):
                line = [load(f, k, n) if axis == 0 else load(f, n, k) for k in range(4)]
                lower = line[0] * DERIV[0][0]
                upper = line[3] * DERIV[3][3]
                for k in range(1, 4):
                    lower = lower + DERIV[0][k] * line[k]
                    upper = upper + DERIV[3][3 - k] * line[3 - k]
                r = face_row(f, n)
                near[r : r + 8, :] = jnp.where(odd, line[0], line[3])
                far[r : r + 8, :] = jnp.where(odd, line[3], line[0])
                wide[wide_at(2 * axis, f, n)] = jnp.where(odd, lower, upper)
                wide[wide_at(2 * axis + 1, f, n)] = jnp.where(odd, upper, lower)
    chosen = selection(coef_ref[PLACE_AT : PLACE_AT + 1, :])
    packed = select(wide[...], chosen, ((1,), (1,)))
    for face in range(4):
        outs[face][FACE:COEF_AT, :] = packed[face * HALF : (face + 1) * HALF]


def by_face(refs, order):
    return tuple(refs[order.index(face)] for face in range(4))


def pack_kernel(t_hbm, base_hbm, flags_hbm, coef_ref, *refs):
    xn, xf, yn, yf = by_face(refs[:4], ORDER_1)
    t_ref, base_ref, flags_ref, wide, sems = refs[4:]
    copies = [
        pltpu.make_async_copy(src, dst, sems.at[k])
        for k, (src, dst) in enumerate(
            ((base_hbm, base_ref), (flags_hbm, flags_ref), (t_hbm, t_ref))
        )
    ]
    for copy in copies:
        copy.start()
    odd_x = lax.axis_index("gx") % 2 == 1
    odd_y = lax.axis_index("gy") % 2 == 1
    copies[0].wait()
    copies[1].wait()
    base_coefs(base_ref, flags_ref, coef_ref)
    copies[2].wait()
    faces = (xn, xf, yn, yf)
    load = lambda f, x, y: tan_in(t_ref, f, x, y)
    pack_faces(load, coef_ref, faces, odd_x, odd_y, wide)
    for axis, (near, far), odd in ((0, (xn, xf), odd_x), (1, (yn, yf), odd_y)):
        for place, name in enumerate(FACE_NAMES + (SX + axis,)):
            first = name * 16
            if axis == 0:
                lower = coef_ref[first : first + 4, :]
                upper = coef_ref[first + 12 : first + 16, :]
            else:
                lower = coef_ref[pl.ds(first, 4, stride=4), :]
                upper = coef_ref[pl.ds(first + 3, 4, stride=4), :]
            r = COEF_AT + 4 * place
            near[r : r + 4, :] = jnp.where(odd, lower, upper)
            far[r : r + 4, :] = jnp.where(odd, upper, lower)
        r = COEF_AT + 28
        near[r : r + 4, :] = coef_ref[PLACE_AT : PLACE_AT + 4, :]
        far[r : r + 4, :] = coef_ref[PLACE_AT : PLACE_AT + 4, :]


def flux(d, t, v, dp, e, hh):
    u = t[1 + d] - v[d] * t[0]
    out = [t[1 + d]]
    for i in range(3):
        value = v[d] * t[1 + i] + v[i] * u
        out.append(value + dp if i == d else value)
    out.append(v[d] * e + hh * u)
    return out


def volume(load, coef_ref, wm_ref, acc, ops, aux, result):
    top_lane = lax.broadcasted_iota(jnp.int32, (COLS, LANES), 1) % 4 == 3
    chunk = 128

    def put(f, x, y, value):
        hi = value.astype(jnp.bfloat16)
        r = row(f, x, y)
        ops[r : r + 16, :LANES] = hi
        ops[r : r + 16, LANES:] = (value - hi.astype(jnp.float32)).astype(jnp.bfloat16)

    def span_product():
        for c in range(640 // chunk):
            both = jnp.dot(
                ops[c * chunk : (c + 1) * chunk, :],
                wm_ref[...],
                preferred_element_type=jnp.float32,
            )
            acc[c * chunk : (c + 1) * chunk, :] = both[:, :LANES] + both[:, LANES:]

    for x in range(4):
        for f in range(5):
            for y in (0, 2):
                put(f, x, y, jnp.concatenate([load(f, x, y), load(f, x, y + 1)], axis=0))
    span_product()

    for x in range(4):
        for y in (0, 2):
            parts = []
            for yy in (y, y + 1):
                t = [load(f, x, yy) for f in range(5)]
                v = [coef(coef_ref, V1 + d, x, yy) for d in range(3)]
                w = [coef(coef_ref, W1 + d, x, yy) for d in range(3)]
                dp = 0.4 * t[4] + coef(coef_ref, KE, x, yy) * t[0]
                for d in range(3):
                    dp = dp - w[d] * t[1 + d]
                e = t[4] + dp
                k = (x * 4 + yy) * 16
                aux[k : k + 8, :] = dp
                aux[k + 8 : k + 16, :] = e
                g = flux(2, t, v, dp, e, coef(coef_ref, HH, x, yy))
                nu = coef(coef_ref, NU, x, yy)
                out = []
                for f in range(5):
                    r = row(f, x, yy)
                    out.append(nu * acc[r : r + 8, :] - g[f])
                parts.append(out)
            for f in range(5):
                put(f, x, y, jnp.concatenate([parts[0][f], parts[1][f]], axis=0))
    span_product()

    for axis in range(2):
        for n in range(4):
            line = [(k, n) if axis == 0 else (n, k) for k in range(4)]
            t = [[load(f, x, y) for f in range(5)] for x, y in line]
            g = []
            for k, (x, y) in enumerate(line):
                v = [coef(coef_ref, V1 + d, x, y) for d in range(3)]
                r = (x * 4 + y) * 16
                g.append(
                    flux(axis, t[k], v, aux[r : r + 8, :], aux[r + 8 : r + 16, :],
                         coef(coef_ref, HH, x, y))
                )
            nu = coef(coef_ref, NU, *line[0])
            for f in range(5):
                tt = [t[k][f] for k in range(4)]
                fl = []
                for i in range(4):
                    fl.append(nu * row_product(i, tt) - g[i][f])
                for i, (x, y) in enumerate(line):
                    r = row(f, x, y)
                    total = acc[r : r + 8, :] + row_product(i, fl)
                    if axis == 0:
                        other = jnp.where(
                            top_lane, pltpu.roll(tt[i], LANES - 1, 1), pltpu.roll(tt[i], 1, 1)
                        )
                        total = total + coef(coef_ref, SZ, x, y) * (other - tt[i])
                    else:
                        total = result(f, x, y, tt[i], total)
                    acc[r : r + 8, :] = total


def row_product(i, values):
    total = None
    for k in range(4):
        if k != i:
            term = DERIV[i][k] * values[k]
            total = term if total is None else total + term
    return total


def add_faces(load, coef_ref, recv, coef_recv, odd_x, odd_y, acc, work, wide, scale, finish):
    for face in range(4):
        r = COEF_AT + 28
        chosen = selection(coef_recv[face][r : r + 1, :])
        wide[face * HALF : (face + 1) * HALF, :] = select(
            recv[face][FACE:COEF_AT, :], chosen, ((1,), (0,))
        )
    for axis, odd in ((0, odd_x), (1, odd_y)):
        near, far = recv[2 * axis : 2 * axis + 2]
        near_c, far_c = coef_recv[2 * axis : 2 * axis + 2]

        def pick(low, r, rows=8):
            a, b = near[r : r + rows, :], far[r : r + rows, :]
            return jnp.where(odd, a, b) if low else jnp.where(odd, b, a)

        def pick_coef(low, place, n):
            r = COEF_AT + 4 * place + n
            a, b = near_c[r : r + 1, :], far_c[r : r + 1, :]
            return jnp.where(odd, a, b) if low else jnp.where(odd, b, a)

        for n in range(4):
            line = [(k, n) if axis == 0 else (n, k) for k in range(4)]
            nu3 = (3.0 * scale) * coef(coef_ref, NU, *line[0])
            shift, extra = [], []
            for low in (True, False):
                place = line[0] if low else line[3]
                far_t = [pick(low, face_row(f, n)) for f in range(5)]
                v = [pick_coef(low, d, n) for d in range(3)]
                dp = 0.4 * far_t[4] + pick_coef(low, 3, n) * far_t[0]
                for d in range(3):
                    dp = dp - (0.4 * v[d]) * far_t[1 + d]
                far_g = flux(axis, far_t, v, dp, far_t[4] + dp, pick_coef(low, 4, n))
                far_nu = pick_coef(low, 5, n)
                s3 = (3.0 * scale) * jnp.maximum(
                    coef(coef_ref, SX + axis, *place), pick_coef(low, 6, n)
                )
                moved, added = [], []
                for f in range(5):
                    gap = far_t[f] - load(f, *place)
                    a = wide[wide_at(2 * axis, f, n)]
                    b = wide[wide_at(2 * axis + 1, f, n)]
                    far_d = jnp.where(odd, a, b) if low else jnp.where(odd, b, a)
                    far_q = far_d - 3.0 * gap if low else far_d + 3.0 * gap
                    value = (3.0 * scale) * (far_nu * far_q - far_g[f])
                    added.append(s3 * gap - value if low else s3 * gap + value)
                    moved.append(-(nu3 * far_t[f]) if low else nu3 * far_t[f])
                shift.append(moved)
                extra.append(added)
            for f in range(5):
                for i, (x, y) in enumerate(line):
                    r = row(f, x, y)
                    total = (acc if axis == 0 else work)[r : r + 8, :]
                    if i != 0:
                        total = total + DERIV[i][0] * shift[0][f]
                    if i != 3:
                        total = total + DERIV[i][3] * shift[1][f]
                    if i == 0:
                        total = total + extra[0][f]
                    if i == 3:
                        total = total + extra[1][f]
                    if axis == 0:
                        work[r : r + 8, :] = total
                    else:
                        finish(f, x, y, total)


def loader(ref):
    def load(f, x, y):
        r = row(f, x, y)
        return ref[r : r + 8, :]

    return load


def first_volume(t_ref, coef_ref, acc, wm_ref, ops, aux):
    span_table(wm_ref)
    volume(
        lambda f, x, y: tan_in(t_ref, f, x, y), coef_ref, wm_ref, acc, ops, aux,
        lambda f, x, y, t, total: t + STEP * total,
    )


def second_volume(t_ref, s_ref, coef_ref, wm_ref, acc, ops, aux):
    def result(f, x, y, s, total):
        return 0.5 * tan_in(t_ref, f, x, y) + (0.5 * s + (0.5 * STEP) * total)

    volume(loader(s_ref), coef_ref, wm_ref, acc, ops, aux, result)


def first_faces(t_ref, coef_ref, acc, r0, r1, r2, r3, s_ref, m0, m1, m2, m3, work, wide):
    odd_x = lax.axis_index("gx") % 2 == 1
    odd_y = lax.axis_index("gy") % 2 == 1
    load = lambda f, x, y: tan_in(t_ref, f, x, y)

    def finish(f, x, y, total):
        r = row(f, x, y)
        s_ref[r : r + 8, :] = total

    faces = by_face((r0, r1, r2, r3), ORDER_1)
    add_faces(load, coef_ref, faces, faces, odd_x, odd_y, acc, work, wide, STEP, finish)
    sent = by_face((m0, m1, m2, m3), ORDER_2)
    pack_faces(loader(s_ref), coef_ref, sent, odd_x, odd_y, wide)


def second_faces(
    s_ref, coef_ref, acc, c0, c1, c2, c3, r0, r1, r2, r3, out_ref, work, wide
):
    odd_x = lax.axis_index("gx") % 2 == 1
    odd_y = lax.axis_index("gy") % 2 == 1
    load = loader(s_ref)

    def finish(f, x, y, total):
        out_ref[pl.ds(f * 16 + x * 4 + y, COLS, stride=80), :] = total

    add_faces(
        load, coef_ref, by_face((r0, r1, r2, r3), ORDER_2),
        by_face((c0, c1, c2, c3), ORDER_1), odd_x, odd_y, acc, work, wide, 0.5 * STEP, finish,
    )


def call(kernel, shapes, scratch, args, flops, space=pltpu.VMEM, limit=16):
    return pl.pallas_call(
        kernel,
        out_shape=[
            s if hasattr(s, "dtype") else jax.ShapeDtypeStruct(s, jnp.float32) for s in shapes
        ],
        in_specs=[pl.BlockSpec(memory_space=space)] * len(args),
        out_specs=[pl.BlockSpec(memory_space=pltpu.VMEM)] * len(shapes),
        scratch_shapes=scratch,
        compiler_params=pltpu.CompilerParams(vmem_limit_bytes=limit * 1024 * 1024),
        cost_estimate=pl.CostEstimate(flops=flops, bytes_accessed=1000000, transcendentals=0),
    )(*args)


def exchange(messages, order):
    size_x, size_y = lax.axis_size("gx"), lax.axis_size("gy")

    def pairs(size, first):
        out = []
        for i in range(first, size - 1, 2):
            out += [(i, i + 1), (i + 1, i)]
        if first == 1:
            out += [(0, 0)]
            if size % 2 == 0:
                out += [(size - 1, size - 1)]
        return out

    plan = (
        ("gx", pairs(size_x, 0)),
        ("gx", pairs(size_x, 1)),
        ("gy", pairs(size_y, 0)),
        ("gy", pairs(size_y, 1)),
    )
    return [lax.ppermute(m, *plan[face]) for m, face in zip(messages, order)]


def per_device(tangent, base_state, shock_flags):
    t = tangent.reshape(640, LANES)
    base = base_state.reshape(80, LANES)
    flags = shock_flags.reshape(1, 32)
    message = (COEF_AT + COEF_ROWS, LANES)
    short = (COEF_AT, LANES)
    whole = (640, LANES)
    volume_scratch = [
        pltpu.VMEM((640, 2 * LANES), jnp.bfloat16),
        pltpu.VMEM((256, LANES), jnp.float32),
    ]
    wide = pltpu.VMEM((4 * HALF, 2 * LANES), jnp.float32)
    work = [pltpu.VMEM(whole, jnp.float32), wide]
    staging = [
        pltpu.VMEM(whole, jnp.float32),
        pltpu.VMEM(base.shape, jnp.float32),
        pltpu.VMEM(flags.shape, jnp.int32),
        wide,
        pltpu.SemaphoreType.DMA((3,)),
    ]
    coefs, *faces = call(
        pack_kernel, [(PLACE_AT + 8, LANES)] + [message] * 4, staging, [t, base, flags], 1000000,
        space=pltpu.HBM, limit=56,
    )
    got = exchange(faces, ORDER_1)
    inner, wm = call(
        first_volume, [whole, jax.ShapeDtypeStruct((256, 256), jnp.bfloat16)], volume_scratch, [t, coefs],
        10000000,
    )
    s, *faces = call(
        first_faces, [whole] + [short] * 4, work, [t, coefs, inner, *got], 1000000
    )
    again = exchange(faces, ORDER_2)
    (inner,) = call(second_volume, [whole], volume_scratch, [t, s, coefs, wm], 10000000)
    (out,) = call(second_faces, [whole], work, [s, coefs, inner, *got, *again], 1000000)
    return out.reshape(tangent.shape)


def solution(mesh):
    in_specs = (P(None, None, "gx", "gy", None), P(None, "gx", "gy", None), P("gx", "gy", None))
    out_specs = P(None, None, "gx", "gy", None)
    return jax.shard_map(
        per_device, mesh=mesh, in_specs=in_specs, out_specs=out_specs, check_vma=False
    )
```
